128 devices in a mesh: brow: 16 (over x_hi, y, core), bcol: 8 (over x_lo, z).
Axes of the slice: x: 4 (x_hi: 2, x_lo: 2; x = x_hi * 2 + x_lo), y: 4, z: 4, core: 2. Of those that a mesh axis runs over, the one named last changes fastest.
Arguments:
- patterns: bfloat16 [2048, 16384], P(('brow', 'bcol')), may hold values from -70 to 70
- components: float32 [16384, 256], P('bcol'), may hold values from -0.046875 to 0.046875
Outputs:
- covariance: float32 [16384, 16384], P('brow', 'bcol')
- projected: float32 [16384, 256], P(('brow', 'bcol'))
- column_means: float32 [16384], P(('brow', 'bcol'))
The draws below stay inside these ranges and needn't reach their ends.
All inputs are finite; a program needn't handle non-finite values.
Results may differ from the reference program's by a relative error of at most 0.0003.
Values may be sent and summed in bfloat16 or wider, within the bound.
No kernel may reach another device: no remote copies, remote signals or barrier semaphores. Data moves between devices by JAX's collectives and lax.ppermute only.
A program may use at most 128 MiB of HBM per device.

```python
import math
import jax
import jax.numpy as jnp
from jax import lax

PIXELS = 16384
COMPS = 256
SCANS = 2048


def draw_patterns(key, part):
    key = jax.random.fold_in(key, 11)
    subkeys = jax.random.split(key, 4)
    position = jnp.arange(SCANS, dtype=jnp.float32) / max(SCANS - 1, 1)
    rising = 3.0 ** position
    jitter = jnp.exp(jax.random.uniform(subkeys[0], (SCANS,), jnp.float32, 0.0, math.log(3.3)))
    amplitude = rising * jitter
    baseline = jax.random.uniform(subkeys[1], (PIXELS,), jnp.float32, 1.0, 3.0)
    pixel_gain = jnp.exp(jax.random.uniform(subkeys[2], (PIXELS,), jnp.float32, 0.0, math.log(10.0)))
    overall = 0.05
    fluctuation = jnp.clip(jax.random.normal(subkeys[3], (SCANS, PIXELS), jnp.float32), -4.0, 4.0)
    correlated = fluctuation + 0.6 * jnp.roll(fluctuation, 1, axis=1) + 0.4 * jnp.roll(fluctuation, 128, axis=1)
    intensity = overall * pixel_gain[None, :] * (baseline[None, :] * rising[:, None] + amplitude[:, None] * correlated)
    return intensity.astype(jnp.bfloat16)


def block_levels(rng, dims, cuts, low, largest):
    def one(axis_at, blocks):
        draws = jax.random.uniform(jax.random.fold_in(jax.random.fold_in(rng, 6), axis_at), (blocks,), jnp.float32, low / len(cuts), largest / len(cuts))
        return jnp.repeat(jnp.exp(draws), dims[axis_at] // blocks).reshape((-1,) + (1,) * (len(dims) - axis_at - 1))

    gain = one(*cuts[0])
    for cut in cuts[1:]:
        gain = gain * one(*cut)
    return gain


def scatter_about(own_key, extent, spread, most, cuts=(), kind=jnp.bfloat16):
    array = spread * jax.random.normal(own_key, extent, jnp.float32)
    if cuts:
        array = array * block_levels(own_key, extent, cuts, -0.22, 0.18)
    return jnp.clip(array, -most, most).astype(kind)


def setup_inputs(seed: int = 0) -> dict:
    keys = jax.random.split(jax.random.key(seed), 3)
    return {
        "patterns": draw_patterns(jax.random.fold_in(keys[2], 71), 0),
        "components": scatter_about(keys[1], (PIXELS, COMPS), PIXELS ** -0.5, 0.046875, ((0, 8),), jnp.float32),
    }


def reference(patterns, components):
    column_sums = jnp.sum(patterns.astype(jnp.float32), axis=0)
    column_means = column_sums / SCANS
    gram = jnp.dot(patterns.T, patterns, preferred_element_type=jnp.float32)
    covariance = (gram - SCANS * column_means[:, None] * column_means[None, :]) / (SCANS - 1)
    projected = jnp.dot(covariance, components, precision=lax.Precision.HIGHEST, preferred_element_type=jnp.float32)
    return covariance, projected, column_means
```

```python
import jax
import jax.numpy as jnp
from jax import lax
from jax.experimental import pallas as pl
from jax.experimental.pallas import tpu as pltpu
from jax.sharding import PartitionSpec as P

F32 = jnp.float32
BF16 = jnp.bfloat16
AXES = ("brow", "bcol")
SCANS = 2048
PIXELS = 16384
COMPS = 256
LOCAL = 16
PANEL = 2048
HALF = 1024
STEPS = (0, 1, -1, 2)
VMEM = pltpu.CompilerParams(vmem_limit_bytes=56 << 20)


def flat(x, y, z, k):
    return (((x // 2) * 4 + y) * 2 + k) * 8 + (x % 2) * 4 + z


def permute(value, move):
    pairs = []
    for x in range(4):
        for y in range(4):
            for z in range(4):
                for k in range(2):
                    x2, y2, z2, k2 = move(x, y, z, k)
                    pairs.append((flat(x, y, z, k), flat(x2, y2 % 4, z2 % 4, k2)))
    return lax.ppermute(value, AXES, pairs)


def spread_same(d):
    return lambda x, y, z, k: (x, y + d, z, k) if k == 0 else (x, y, z + d, k)


def spread_cross(d):
    return lambda x, y, z, k: (x, y, z + d, 1) if k == 0 else (x, y + d, z, 0)


def across(m):
    return lambda x, y, z, k: (x ^ m, y, z, k)


def around(d):
    return lambda x, y, z, k: (x, y, z + d, k) if k == 0 else (x, y + d, z, k)


def pick_kernel(at, patterns, *pieces):
    for n, piece in enumerate(pieces):
        for half in range(2):
            start = pl.multiple_of((half * 4 + at[n]) * PANEL, PANEL)
            piece[half] = patterns[:, pl.ds(start, PANEL)]


def pick(at, patterns):
    piece = jax.ShapeDtypeStruct((2, LOCAL, PANEL), BF16)
    return pl.pallas_call(
        pick_kernel,
        out_shape=[piece] * 8,
        in_specs=[pl.BlockSpec(memory_space=pltpu.SMEM), pl.BlockSpec(memory_space=pltpu.VMEM)],
        out_specs=[pl.BlockSpec(memory_space=pltpu.VMEM)] * 8,
        compiler_params=VMEM,
    )(at, patterns)


def group_kernel(at, *refs):
    pieces, groups = refs[:8], refs[8:]
    for n, group in enumerate(groups):
        half = at[n]
        for i, piece in enumerate(pieces):
            group[i] = piece[half]


def group(at, pieces):
    whole = jax.ShapeDtypeStruct((8, LOCAL, PANEL), BF16)
    return pl.pallas_call(
        group_kernel,
        out_shape=[whole] * 4,
        in_specs=[pl.BlockSpec(memory_space=pltpu.SMEM)] + [pl.BlockSpec(memory_space=pltpu.VMEM)] * 8,
        out_specs=[pl.BlockSpec(memory_space=pltpu.VMEM)] * 4,
        compiler_params=VMEM,
    )(at, *pieces)


def fetch(core, own, recv, rows, cols, sems):
    def start(row_from, col_from, first):
        for m in range(4):
            pltpu.make_async_copy(col_from[m], cols.at[m], sems.at[m]).start()
            for s in range(2):
                for dy in range(4):
                    pltpu.make_async_copy(
                        row_from[m].at[:, s, dy, :, pl.ds(first, HALF)], rows.at[m, dy, 1 - s], sems.at[m]
                    ).start()

    @pl.when(core == 0)
    def _():
        start(own, recv, 0)

    @pl.when(core == 1)
    def _():
        start(recv, own, HALF)


def fetched(own, rows, cols, sems, m):
    pltpu.make_async_copy(own[m], cols.at[m], sems.at[m]).wait()
    for s in range(2):
        for dy in range(4):
            pltpu.make_async_copy(
                own[m].at[:, s, dy, :, pl.ds(0, HALF)], rows.at[m, dy, 1 - s], sems.at[m]
            ).wait()


def project_kernel(at, *refs):
    own, recv, comps, parts = refs[:4], refs[4:8], refs[8], refs[9:13]
    rows, cols, high, low, scores, sems = refs[13:]
    fetch(at[4], own, recv, rows, cols, sems)
    value = comps[...]
    high[...] = value.astype(BF16)
    low[...] = (value - high[...].astype(F32)).astype(BF16)
    total = jnp.zeros((1, COMPS), F32)
    for m in range(4):
        fetched(own, rows, cols, sems, m)
        block = cols[m].reshape(512, PANEL)
        score = jnp.dot(block, high[...], preferred_element_type=F32) + jnp.dot(
            block, low[...], preferred_element_type=F32
        )
        scores[pl.ds(m * 512, 512), :] = score
        total += jnp.sum(score, axis=0, keepdims=True)
    centred = scores[...] - total / SCANS
    upper = centred.astype(BF16)
    lower = (centred - upper.astype(F32)).astype(BF16)
    panel = rows[...].reshape(SCANS, HALF)
    dims = (((0,), (0,)), ((), ()))
    result = lax.dot_general(upper, panel, dims, preferred_element_type=F32) + lax.dot_general(
        lower, panel, dims, preferred_element_type=F32
    )
    result = result / (SCANS - 1)
    for c in range(8):
        cell = result[:, c * 128 : (c + 1) * 128]
        xl, z = c // 4, c % 4
        for n in range(4):

            @pl.when(at[n] == z)
            def _():
                parts[n][xl] = cell


def project(at, own, recv, comps):
    part = jax.ShapeDtypeStruct((2, COMPS, 128), F32)
    return pl.pallas_call(
        project_kernel,
        out_shape=[part] * 4,
        in_specs=[pl.BlockSpec(memory_space=pltpu.SMEM)]
        + [pl.BlockSpec(memory_space=pl.ANY)] * 8
        + [pl.BlockSpec(memory_space=pltpu.VMEM)],
        out_specs=[pl.BlockSpec(memory_space=pltpu.VMEM)] * 4,
        scratch_shapes=[
            pltpu.VMEM((4, 4, 2, 4, LOCAL, HALF), BF16),
            pltpu.VMEM((4, 4, 2, 4, LOCAL, PANEL), BF16),
            pltpu.VMEM((PANEL, COMPS), BF16),
            pltpu.VMEM((PANEL, COMPS), BF16),
            pltpu.VMEM((SCANS, COMPS), F32),
            pltpu.SemaphoreType.DMA((4,)),
        ],
        compiler_params=VMEM,
        cost_estimate=pl.CostEstimate(flops=6 << 30, bytes_accessed=14 << 20, transcendentals=0),
    )(at, *own, *recv, comps)


def gram_kernel(at, *refs):
    own, recv, out, means = refs[:4], refs[4:8], refs[8], refs[9]
    rows, cols, row_sums, col_sums, stage, sems, out_sems = refs[10:]
    fetch(at[4], own, recv, rows, cols, sems)
    row_sums[...] = jnp.zeros_like(row_sums)
    col_sums[...] = jnp.zeros_like(col_sums)
    for m in range(4):
        fetched(own, rows, cols, sems, m)
        for a in range(4):
            row_sums[...] += jnp.sum(rows[m, a].reshape(128, HALF).astype(F32), axis=0, keepdims=True)
            col_sums[...] += jnp.sum(cols[m, a].reshape(128, PANEL).astype(F32), axis=0, keepdims=True)
    row_sums[...] = row_sums[...] / SCANS
    means[...] = row_sums[...]
    dims = (((0,), (0,)), ((), ()))
    copies = []
    for i in range(4):
        slot = i % 2
        if i >= 2:
            copies[i - 2].wait()
        left = rows[:, :, :, :, :, i * 256 : (i + 1) * 256].reshape(SCANS, 256)
        row_mean = jnp.transpose(jnp.broadcast_to(row_sums[:, i * 256 : (i + 1) * 256], (128, 256)))[:, :1]
        for j in range(8):
            span = slice(j * 256, (j + 1) * 256)
            right = cols[:, :, :, :, :, span].reshape(SCANS, 256)
            tile = lax.dot_general(left, right, dims, preferred_element_type=F32)
            stage[slot, :, span] = (tile - row_mean * col_sums[:, span]) * (1.0 / (SCANS - 1))
        copy = pltpu.make_async_copy(stage.at[slot], out.at[pl.ds(i * 256, 256), :], out_sems.at[slot])
        copy.start()
        copies.append(copy)
    copies[2].wait()
    copies[3].wait()


def gram(at, own, recv):
    return pl.pallas_call(
        gram_kernel,
        out_shape=[jax.ShapeDtypeStruct((HALF, PANEL), F32), jax.ShapeDtypeStruct((1, HALF), F32)],
        in_specs=[pl.BlockSpec(memory_space=pltpu.SMEM)] + [pl.BlockSpec(memory_space=pl.ANY)] * 8,
        out_specs=[pl.BlockSpec(memory_space=pl.ANY), pl.BlockSpec(memory_space=pltpu.VMEM)],
        scratch_shapes=[
            pltpu.VMEM((4, 4, 2, 4, LOCAL, HALF), BF16),
            pltpu.VMEM((4, 4, 2, 4, LOCAL, PANEL), BF16),
            pltpu.VMEM((1, HALF), F32),
            pltpu.VMEM((1, PANEL), F32),
            pltpu.VMEM((2, 256, PANEL), F32),
            pltpu.SemaphoreType.DMA((4,)),
            pltpu.SemaphoreType.DMA((2,)),
        ],
        compiler_params=VMEM,
        cost_estimate=pl.CostEstimate(flops=8 << 30, bytes_accessed=20 << 20, transcendentals=0),
    )(at, *own, *recv)


def on_device(patterns, components):
    row = lax.axis_index("brow")
    col = lax.axis_index("bcol")
    k, y, xh = row % 2, (row // 2) % 4, row // 8
    z, xl = col % 4, col // 4
    first = k == 0
    same = jnp.where(first, y, z)
    cross = jnp.where(first, z, y)
    at = jnp.stack([(same + d) % 4 for d in STEPS] + [(cross + d) % 4 for d in STEPS]).astype(jnp.int32)
    sends = pick(at, patterns)
    got = [sends[0]]
    got += [permute(sends[n], spread_same(STEPS[n])) for n in range(1, 4)]
    got += [permute(sends[4 + n], spread_cross(STEPS[n])) for n in range(4)]
    own_half = jnp.where(first, xh, xl)
    at = jnp.stack(
        [own_half, jnp.where(first, own_half, 1 - own_half), jnp.where(first, 1 - own_half, own_half), 1 - own_half]
    ).astype(jnp.int32)
    sends = group(at, got)
    groups = [sends[0]] + [permute(sends[m], across(m)) for m in (1, 2, 3)]
    own, recv = [], []
    for g in groups:
        whole = jnp.stack([g] + [permute(g, around(d)) for d in STEPS[1:]])
        whole = whole.reshape(4, 2, 4, LOCAL, PANEL)
        own.append(whole)
        recv.append(permute(whole, lambda x, y, z, k: (x, y, z, 1 - k)))
    at = jnp.stack([(z + d) % 4 for d in STEPS] + [k]).astype(jnp.int32)
    parts = project(at, own, recv, components)
    ring = [parts[0]] + [permute(parts[n], lambda x, y, z, k, d=STEPS[n]: (x, y, z + d, k)) for n in range(1, 4)]
    covariance, means = gram(at, own, recv)
    part = ring[0] + ring[1] + ring[2] + ring[3]
    mine = lax.dynamic_index_in_dim(part, xl, 0, keepdims=False)
    theirs = lax.dynamic_index_in_dim(part, 1 - xl, 0, keepdims=False)
    projected = (mine + permute(theirs, across(1))).T
    means_part = lax.dynamic_slice_in_dim(means[0], col * 128, 128, 0)
    return covariance, projected, means_part


def solution(mesh):
    return jax.shard_map(
        on_device,
        mesh=mesh,
        in_specs=(P(("brow", "bcol"), None), P("bcol", None)),
        out_specs=(P("brow", "bcol"), P(("brow", "bcol"), None), P(("brow", "bcol"))),
        check_vma=False,
    )
```

```python
import functools

import jax
import jax.numpy as jnp
from jax import lax
from jax.experimental import pallas as pl
from jax.experimental.pallas import tpu as pltpu
from jax.sharding import PartitionSpec as P

F32 = jnp.float32
BF16 = jnp.bfloat16
AXES = ("brow", "bcol")
SCANS = 2048
PIXELS = 16384
COMPS = 256
LOCAL = 16
PANEL = 2048
HALF = 1024
STEPS = (0, 1, -1, 2)
VMEM = pltpu.CompilerParams(vmem_limit_bytes=56 << 20)


def flat(x, y, z, k):
    return (((x // 2) * 4 + y) * 2 + k) * 8 + (x % 2) * 4 + z


def permute(value, move):
    pairs = []
    for x in range(4):
        for y in range(4):
            for z in range(4):
                for k in range(2):
                    x2, y2, z2, k2 = move(x, y, z, k)
                    pairs.append((flat(x, y, z, k), flat(x2, y2 % 4, z2 % 4, k2)))
    return lax.ppermute(value, AXES, pairs)


def spread_same(d):
    return lambda x, y, z, k: (x, y + d, z, k) if k == 0 else (x, y, z + d, k)


def spread_cross(d):
    return lambda x, y, z, k: (x, y, z + d, 1) if k == 0 else (x, y + d, z, 0)


def across(m):
    return lambda x, y, z, k: (x ^ m, y, z, k)


def around(d):
    return lambda x, y, z, k: (x, y, z + d, k) if k == 0 else (x, y + d, z, k)


def pick_kernel(at, patterns, *pieces):
    for n, piece in enumerate(pieces):
        for half in range(2):
            start = pl.multiple_of((half * 4 + at[n]) * PANEL, PANEL)
            piece[half] = patterns[:, pl.ds(start, PANEL)]


def pick(at, patterns):
    piece = jax.ShapeDtypeStruct((2, LOCAL, PANEL), BF16)
    return pl.pallas_call(
        pick_kernel,
        out_shape=[piece] * 8,
        in_specs=[pl.BlockSpec(memory_space=pltpu.SMEM), pl.BlockSpec(memory_space=pltpu.VMEM)],
        out_specs=[pl.BlockSpec(memory_space=pltpu.VMEM)] * 8,
        compiler_params=VMEM,
    )(at, patterns)


def group_kernel(at, *refs):
    pieces, groups = refs[:8], refs[8:]
    for n, group in enumerate(groups):
        half = at[n]
        for i, piece in enumerate(pieces):
            group[i] = piece[half]


def group(at, pieces):
    whole = jax.ShapeDtypeStruct((8, LOCAL, PANEL), BF16)
    return pl.pallas_call(
        group_kernel,
        out_shape=[whole] * 4,
        in_specs=[pl.BlockSpec(memory_space=pltpu.SMEM)] + [pl.BlockSpec(memory_space=pltpu.VMEM)] * 8,
        out_specs=[pl.BlockSpec(memory_space=pltpu.VMEM)] * 4,
        compiler_params=VMEM,
    )(at, *pieces)


def fetch(core, members, rows, cols, sems, row_first=0, row_width=HALF, only_rows=()):
    def start(by_core, offset):
        for own, recv, m, step in members:
            row_from, col_from = (own, recv) if by_core == 0 else (recv, own)
            if m not in only_rows:
                pltpu.make_async_copy(col_from, cols.at[m, step], sems.at[m]).start()
            for s in range(2):
                pltpu.make_async_copy(
                    row_from.at[s, :, :, pl.ds(offset, row_width)], rows.at[m, :, 1 - s, step], sems.at[m]
                ).start()

    @pl.when(core == 0)
    def _():
        start(0, row_first)

    @pl.when(core == 1)
    def _():
        start(1, HALF + row_first)


def fetched(members, rows, cols, sems, which, row_width=HALF, only_rows=()):
    for own, recv, m, step in members:
        if m == which:
            if m not in only_rows:
                pltpu.make_async_copy(own, cols.at[m, step], sems.at[m]).wait()
            for s in range(2):
                pltpu.make_async_copy(
                    own.at[s, :, :, pl.ds(0, row_width)], rows.at[m, :, 1 - s, step], sems.at[m]
                ).wait()


def views(own, recv, shapes):
    members = []
    for a, b, (groups, steps) in zip(own, recv, shapes):
        for i, m in enumerate(groups):
            for j, step in enumerate(steps):
                members.append((a.at[i, j], b.at[i, j], m, step))
    return members


SHAPE_OWN = [((0,), (0, 1, 2, 3))]
SHAPE_NEAR = [((1, 2), (n,)) for n in range(4)]
SHAPE_FAR = [((3,), (n,)) for n in range(4)]
ANY = pl.BlockSpec(memory_space=pl.ANY)
IN_VMEM = pl.BlockSpec(memory_space=pltpu.VMEM)
IN_SMEM = pl.BlockSpec(memory_space=pltpu.SMEM)
ROWS = pltpu.VMEM((4, 4, 2, 4, LOCAL, HALF), BF16)
COLS = pltpu.VMEM((4, 4, 2, 4, LOCAL, PANEL), BF16)


LEFT = (((0,), (0,)), ((), ()))


def ones_beside(block):
    return jnp.concatenate([block, jnp.ones((block.shape[0], 128), BF16)], axis=1)


def early_kernel(shapes, first, last, at, *refs):
    count = len(shapes)
    own, recv, comps = refs[:count], refs[count : 2 * count], refs[2 * count]
    refs = refs[2 * count + 1 :]
    if not first:
        t_in, rs_in, ys_in, origin_in = refs[:4]
        refs = refs[4:]
    if last:
        parts, means = refs[:2]
        refs = refs[2:]
    else:
        t_out, rs_out, ys_out, origin_out = refs[:4]
        refs = refs[4:]
    rows, cols, sems = refs
    members = views(own, recv, shapes)
    groups = sorted({member[2] for member in members})
    low = groups[0]
    members = [(a, b, m - low, step) for a, b, m, step in members]
    fetch(at[4], members, rows, cols, sems)
    total = jnp.zeros((COMPS, HALF), F32) if first else t_in[...]
    row_sum = jnp.zeros((1, HALF), F32) if first else rs_in[...]
    score_sum = jnp.zeros((1, COMPS), F32) if first else ys_in[...]
    origin = None if first else origin_in[...]
    for m in range(len(groups)):
        fetched(members, rows, cols, sems, m)
        score = jnp.dot(cols[m].reshape(512, PANEL), comps[...], preferred_element_type=F32)
        score = score[:, :COMPS] + score[:, COMPS:]
        added = jnp.sum(score, axis=0, keepdims=True)
        score_sum = score_sum + added
        if origin is None:
            origin = added / 512
        centred = score - origin
        high = centred.astype(BF16)
        lower = (centred - high.astype(F32)).astype(BF16)
        left = ones_beside(jnp.concatenate([high, lower], axis=1))
        product = lax.dot_general(left, rows[m].reshape(512, HALF), LEFT, preferred_element_type=F32)
        total = total + (product[:COMPS] + product[COMPS : 2 * COMPS])
        row_sum = row_sum + product[2 * COMPS : 2 * COMPS + 1]
    if last:
        shift = score_sum / SCANS - origin
        shift = jnp.transpose(jnp.broadcast_to(shift, (128, COMPS)))[:, :1]
        total = (total - shift * row_sum) * (1.0 / (SCANS - 1))
        for c in range(8):
            parts[c] = total[:, c * 128 : (c + 1) * 128]
        means[...] = row_sum * (1.0 / SCANS)
    else:
        t_out[...] = total
        rs_out[...] = row_sum
        ys_out[...] = score_sum
        origin_out[...] = origin


def early(at, own, recv, shapes, comps, before=(), last=False):
    count = len(own)
    groups = len({m for groups, _ in shapes for m in groups})
    state = [
        jax.ShapeDtypeStruct((COMPS, HALF), F32),
        jax.ShapeDtypeStruct((1, HALF), F32),
        jax.ShapeDtypeStruct((1, COMPS), F32),
        jax.ShapeDtypeStruct((1, COMPS), F32),
    ]
    result = [jax.ShapeDtypeStruct((8, COMPS, 128), F32), jax.ShapeDtypeStruct((1, HALF), F32)]
    return pl.pallas_call(
        functools.partial(early_kernel, shapes, not before, last),
        out_shape=result if last else state,
        in_specs=[IN_SMEM] + [ANY] * (2 * count) + [IN_VMEM] * (1 + len(before)),
        out_specs=[IN_VMEM] * (2 if last else 4),
        scratch_shapes=[
            pltpu.VMEM((groups, 4, 2, 4, LOCAL, HALF), BF16),
            pltpu.VMEM((groups, 4, 2, 4, LOCAL, PANEL), BF16),
            pltpu.SemaphoreType.DMA((4,)),
        ],
        compiler_params=pltpu.CompilerParams(vmem_limit_bytes=28 << 20),
        cost_estimate=pl.CostEstimate(flops=(2 * groups) << 30, bytes_accessed=(4 * groups) << 20, transcendentals=0),
    )(at, *own, *recv, comps, *before)


def gram_kernel(at, *refs):
    own, recv, row_means, out = refs[:9], refs[9:18], refs[18], refs[19]
    rows, cols, stage, col_sums, sems, out_sems = refs[20:]
    members = views(own, recv, SHAPE_OWN + SHAPE_NEAR + SHAPE_FAR)
    fetch(at[4], members, rows, cols, sems)
    copies = []
    for i in range(4):
        slot = i % 2
        if i >= 2:
            copies[i - 2].wait()
        span_i = slice(i * 256, (i + 1) * 256)
        row_mean = jnp.transpose(jnp.broadcast_to(row_means[:, span_i], (128, 256)))[:, :1]
        if i == 0:
            for m in range(4):
                fetched(members, rows, cols, sems, m)
                left = ones_beside(rows[m, :, :, :, :, span_i].reshape(512, 256))
                for j in range(8):
                    span = slice(j * 256, (j + 1) * 256)
                    right = cols[m, :, :, :, :, span].reshape(512, 256)
                    both = lax.dot_general(left, right, LEFT, preferred_element_type=F32)
                    tile, col_sum = both[:256], both[256:257]
                    if m > 0:
                        tile += stage[slot, :, span]
                        col_sum += col_sums[:, span]
                    if m == 3:
                        tile = (tile - row_mean * col_sum) * (1.0 / (SCANS - 1))
                    stage[slot, :, span] = tile
                    col_sums[:, span] = col_sum
        else:
            left = rows[:, :, :, :, :, span_i].reshape(SCANS, 256)
            for j in range(8):
                span = slice(j * 256, (j + 1) * 256)
                right = cols[:, :, :, :, :, span].reshape(SCANS, 256)
                tile = lax.dot_general(left, right, LEFT, preferred_element_type=F32)
                stage[slot, :, span] = (tile - row_mean * col_sums[:, span]) * (1.0 / (SCANS - 1))
        copy = pltpu.make_async_copy(stage.at[slot], out.at[pl.ds(i * 256, 256), :], out_sems.at[slot])
        copy.start()
        copies.append(copy)
    for copy in copies[2:]:
        copy.wait()


def gram(at, own, recv, row_means):
    return pl.pallas_call(
        gram_kernel,
        out_shape=jax.ShapeDtypeStruct((HALF, PANEL), F32),
        in_specs=[IN_SMEM] + [ANY] * 18 + [IN_VMEM],
        out_specs=ANY,
        scratch_shapes=[
            ROWS,
            COLS,
            pltpu.VMEM((2, 256, PANEL), F32),
            pltpu.VMEM((1, PANEL), F32),
            pltpu.SemaphoreType.DMA((4,)),
            pltpu.SemaphoreType.DMA((2,)),
        ],
        compiler_params=pltpu.CompilerParams(vmem_limit_bytes=30 << 20),
        cost_estimate=pl.CostEstimate(flops=8 << 30, bytes_accessed=20 << 20, transcendentals=0),
    )(at, *[pltpu.with_memory_space_constraint(piece, pltpu.HBM) for piece in own + recv], row_means)


def on_device(patterns, components):
    row = lax.axis_index("brow")
    col = lax.axis_index("bcol")
    k, y, xh = row % 2, (row // 2) % 4, row // 8
    z, xl = col % 4, col // 4
    first = k == 0
    same = jnp.where(first, y, z)
    cross = jnp.where(first, z, y)
    at = jnp.stack([(same + d) % 4 for d in STEPS] + [(cross + d) % 4 for d in STEPS]).astype(jnp.int32)
    sends = pick(at, patterns)
    got = [sends[0]]
    got += [permute(sends[n], spread_same(STEPS[n])) for n in range(1, 4)]
    got += [permute(sends[4 + n], spread_cross(STEPS[n])) for n in range(4)]
    own_half = jnp.where(first, xh, xl)
    at = jnp.stack(
        [own_half, jnp.where(first, own_half, 1 - own_half), jnp.where(first, 1 - own_half, own_half), 1 - own_half]
    ).astype(jnp.int32)
    sends = group(at, got)
    shape = (2, 4, LOCAL, PANEL)
    swap = lambda x, y, z, k: (x, y, z, 1 - k)
    high = lax.reduce_precision(components, 8, 7)
    comps = jnp.concatenate([high, components - high], axis=1).astype(BF16)
    group_own = sends[0]
    near = [permute(sends[1], across(1)), permute(sends[3], across(3))]
    ring_own = [permute(group_own, around(d)) for d in STEPS[1:]]
    late, ring_own = lax.optimization_barrier((sends[2], ring_own))
    far = permute(late, across(2))
    own = [jnp.stack([group_own] + ring_own).reshape((1, 4) + shape)]
    recv = [permute(own[0], swap)]
    recv, far = lax.optimization_barrier((recv, far))
    at = jnp.stack([k] * 5).astype(jnp.int32)
    group_near = jnp.stack(near)
    ring_near = [group_near] + [permute(group_near, around(d)) for d in STEPS[1:]]
    own_near = [r.reshape((2, 1) + shape) for r in ring_near]
    state = early(at, own, recv, SHAPE_OWN, comps)
    far, ring_near[1:], state = lax.optimization_barrier((far, ring_near[1:], state))
    recv_near = [permute(r, swap) for r in own_near]
    ring_far = [far] + [permute(far, around(d)) for d in STEPS[1:]]
    own_far = [r.reshape((1, 1) + shape) for r in ring_far]
    state = early(at, own_near, recv_near, SHAPE_NEAR, comps, state)
    recv_far = [permute(r, swap) for r in own_far]
    parts, row_means = early(at, own_far, recv_far, SHAPE_FAR, comps, state, True)
    own = own + own_near + own_far
    recv = recv + recv_near + recv_far
    parts = lax.all_to_all(parts, "bcol", 0, 0, tiled=True)
    covariance = gram(at, own, recv, row_means)
    projected = jnp.sum(parts, axis=0).T
    means_part = lax.dynamic_slice_in_dim(row_means[0], col * 128, 128, 0)
    return covariance, projected, means_part


def solution(mesh):
    return jax.shard_map(
        on_device,
        mesh=mesh,
        in_specs=(P(("brow", "bcol"), None), P("bcol", None)),
        out_specs=(P("brow", "bcol"), P(("brow", "bcol"), None), P(("brow", "bcol"))),
        check_vma=False,
    )
```

```python
import functools

import jax
import jax.numpy as jnp
from jax import lax
from jax.experimental import pallas as pl
from jax.experimental.pallas import tpu as pltpu
from jax.sharding import PartitionSpec as P

F32 = jnp.float32
BF16 = jnp.bfloat16
AXES = ("brow", "bcol")
SCANS = 2048
PIXELS = 16384
COMPS = 256
LOCAL = 16
PANEL = 2048
HALF = 1024
STEPS = (0, 1, -1, 2)
ANY = pl.BlockSpec(memory_space=pl.ANY)
IN_VMEM = pl.BlockSpec(memory_space=pltpu.VMEM)
IN_SMEM = pl.BlockSpec(memory_space=pltpu.SMEM)
MIDDLE = pltpu.CompilerParams(vmem_limit_bytes=24 << 20)
SMALL = pltpu.CompilerParams(vmem_limit_bytes=8 << 20)


def flat(x, y, z, k):
    return (((x // 2) * 4 + y) * 2 + k) * 8 + (x % 2) * 4 + z


def permute(value, move):
    pairs = []
    for x in range(4):
        for y in range(4):
            for z in range(4):
                for k in range(2):
                    x2, y2, z2, k2 = move(x, y, z, k)
                    pairs.append((flat(x, y, z, k), flat(x2, y2 % 4, z2 % 4, k2)))
    return lax.ppermute(value, AXES, pairs)


def spread(d):
    return lambda x, y, z, k: (x, y + d, z, k) if k == 0 else (x, y, z + d, k)


def across(m):
    return lambda x, y, z, k: (x ^ m, y, z, k)


def around(d):
    return lambda x, y, z, k: (x, y, z + d, k) if k == 0 else (x, y + d, z, k)


def swap(x, y, z, k):
    return x, y, z, 1 - k


def pick_kernel(at, mine, other, *pieces):
    for n, piece in enumerate(pieces):
        for half in range(2):
            span = pl.ds(pl.multiple_of((half * 4 + at[n]) * PANEL, PANEL), PANEL)
            piece[half, 0] = mine[:, span]
            piece[half, 1] = other[:, span]


def pick(at, mine, other):
    return pl.pallas_call(
        pick_kernel,
        out_shape=[jax.ShapeDtypeStruct((2, 2, LOCAL, PANEL), BF16)] * 4,
        in_specs=[IN_SMEM] + [IN_VMEM] * 2,
        out_specs=[IN_VMEM] * 4,
        compiler_params=SMALL,
    )(at, mine, other)


def group_kernel(at, *refs):
    pieces, groups = refs[:4], refs[4:]
    for n, group in enumerate(groups):
        for i, piece in enumerate(pieces):
            for source in range(2):
                group[source, i] = piece[at[n], source]


def group(at, pieces):
    return pl.pallas_call(
        group_kernel,
        out_shape=[jax.ShapeDtypeStruct((2, 4, LOCAL, PANEL), BF16)] * 4,
        in_specs=[IN_SMEM] + [IN_VMEM] * 4,
        out_specs=[IN_VMEM] * 4,
        compiler_params=SMALL,
    )(at, *pieces)


OWN = tuple((0, step) for step in range(4))
SOON = ((1, 0), (2, 0), (1, 1), (2, 1), (1, 2), (2, 2), (3, 0))
LATE = ((1, 3), (3, 1), (2, 3), (3, 2), (3, 3))
ORDER = (OWN, SOON, LATE)
LEFT = (((0,), (0,)), ((), ()))


def fetch(core, own, recv, rows, cols, sems):
    def start(row_from, col_from, offset):
        for row, col, labels in zip(row_from, col_from, ORDER):
            for i, (m, step) in enumerate(labels):
                pltpu.make_async_copy(col.at[i], cols.at[m, step], sems.at[m]).start()
                for s in range(2):
                    pltpu.make_async_copy(
                        row.at[i, s, :, :, pl.ds(offset, HALF)], rows.at[m, :, 1 - s, step], sems.at[m]
                    ).start()

    @pl.when(core == 0)
    def _():
        start(own, recv, 0)

    @pl.when(core == 1)
    def _():
        start(recv, own, HALF)


def fetched(own, rows, cols, sems, which):
    for array, labels in zip(own, ORDER):
        for i, (m, step) in enumerate(labels):
            if m == which:
                pltpu.make_async_copy(array.at[i], cols.at[m, step], sems.at[m]).wait()
                for s in range(2):
                    pltpu.make_async_copy(
                        array.at[i, s, :, :, pl.ds(0, HALF)], rows.at[m, :, 1 - s, step], sems.at[m]
                    ).wait()


ROWS = pltpu.VMEM((4, 4, 2, 4, LOCAL, HALF), BF16)
COLS = pltpu.VMEM((4, 4, 2, 4, LOCAL, PANEL), BF16)


def ones_beside(block):
    return jnp.concatenate([block, jnp.ones((block.shape[0], 128), BF16)], axis=1)


def score_of(block, comps):
    score = jnp.dot(block, comps, preferred_element_type=F32)
    return score[:, :COMPS] + score[:, COMPS:]


def select(core, own, recv, use):
    @pl.when(core == 0)
    def _():
        use(own, recv, 0)

    @pl.when(core == 1)
    def _():
        use(recv, own, HALF)


def left_of(centred):
    high = centred.astype(BF16)
    low = (centred - high.astype(F32)).astype(BF16)
    return ones_beside(jnp.concatenate([high, low], axis=1))


def product_of(left, panel):
    product = lax.dot_general(left, panel, LEFT, preferred_element_type=F32)
    return product[:COMPS] + product[COMPS : 2 * COMPS], product[2 * COMPS : 2 * COMPS + 1]


def own_kernel(at, own, recv, comps, total, row_sum, score_sum, origin, rows, cols):
    def use(row_from, col_from, offset):
        for i in range(4):
            cols[i] = col_from[i]
            for s in range(2):
                rows[:, 1 - s, i] = row_from[i, s, :, :, offset : offset + HALF]

    select(at[0], own, recv, use)
    score = score_of(cols[...].reshape(512, PANEL), comps[...])
    score_sum[...] = jnp.sum(score, axis=0, keepdims=True)
    origin[...] = score_sum[...] * (1.0 / 512)
    total[...], row_sum[...] = product_of(left_of(score - origin[...]), rows[...].reshape(512, HALF))


def own_part(at, own, recv, comps):
    return pl.pallas_call(
        own_kernel,
        out_shape=[
            jax.ShapeDtypeStruct((COMPS, HALF), F32),
            jax.ShapeDtypeStruct((1, HALF), F32),
            jax.ShapeDtypeStruct((1, COMPS), F32),
            jax.ShapeDtypeStruct((1, COMPS), F32),
        ],
        in_specs=[IN_SMEM] + [IN_VMEM] * 3,
        out_specs=[IN_VMEM] * 4,
        scratch_shapes=[
            pltpu.VMEM((4, 2, 4, LOCAL, HALF), BF16),
            pltpu.VMEM((4, 2, 4, LOCAL, PANEL), BF16),
        ],
        compiler_params=MIDDLE,
        cost_estimate=pl.CostEstimate(flops=2 << 30, bytes_accessed=1 << 20, transcendentals=0),
    )(at, own, recv, comps)


def soon_kernel(at, own, recv, comps, scores, cols):
    def use(row_from, col_from, offset):
        for i in range(len(SOON)):
            cols[i] = col_from[i]

    select(at[0], own, recv, use)
    scores[...] = score_of(cols[...].reshape(len(SOON) * 128, PANEL), comps[...])


def soon_part(at, own, recv, comps):
    return pl.pallas_call(
        soon_kernel,
        out_shape=jax.ShapeDtypeStruct((len(SOON) * 128, COMPS), F32),
        in_specs=[IN_SMEM] + [IN_VMEM] * 3,
        out_specs=IN_VMEM,
        scratch_shapes=[pltpu.VMEM((len(SOON), 2, 4, LOCAL, PANEL), BF16)],
        compiler_params=MIDDLE,
        cost_estimate=pl.CostEstimate(flops=2 << 30, bytes_accessed=1 << 20, transcendentals=0),
    )(at, own, recv, comps)


def last_kernel(at, *refs):
    own_soon, recv_soon, own_late, recv_late, comps, soon, total_in, rs_in, ss_in, origin_in = refs[:10]
    parts, means, rows, cols, left = refs[10:]

    def use(row_from, col_from, offset):
        for array, labels in zip(row_from, (SOON, LATE)):
            for i, (m, step) in enumerate(labels):
                for s in range(2):
                    rows[m - 1, :, 1 - s, step] = array[i, s, :, :, offset : offset + HALF]
        for i in range(len(LATE)):
            cols[i] = col_from[1][i]

    select(at[0], (own_soon, own_late), (recv_soon, recv_late), use)
    late = score_of(cols[...].reshape(len(LATE) * 128, PANEL), comps[...])
    score_sum = ss_in[...] + jnp.sum(late, axis=0, keepdims=True) + jnp.sum(soon[...], axis=0, keepdims=True)
    origin = origin_in[...]
    for block, labels in ((soon[...], SOON), (late, LATE)):
        block = left_of(block - origin)
        for i, (m, step) in enumerate(labels):
            left[pl.ds(((m - 1) * 4 + step) * 128, 128), :] = block[i * 128 : (i + 1) * 128]
    total, row_sum = product_of(left[...], rows[...].reshape(1536, HALF))
    row_sum = row_sum + rs_in[...]
    shift = score_sum * (1.0 / SCANS) - origin
    shift = jnp.transpose(jnp.broadcast_to(shift, (128, COMPS)))[:, :1]
    total = (total + total_in[...] - shift * row_sum) * (1.0 / (SCANS - 1))
    for c in range(8):
        parts[c] = total[:, c * 128 : (c + 1) * 128]
    means[...] = row_sum * (1.0 / SCANS)


def last_part(at, pieces, comps, soon, state):
    return pl.pallas_call(
        last_kernel,
        out_shape=[jax.ShapeDtypeStruct((8, COMPS, 128), F32), jax.ShapeDtypeStruct((1, HALF), F32)],
        in_specs=[IN_SMEM] + [IN_VMEM] * 10,
        out_specs=[IN_VMEM] * 2,
        scratch_shapes=[
            pltpu.VMEM((3, 4, 2, 4, LOCAL, HALF), BF16),
            pltpu.VMEM((len(LATE), 2, 4, LOCAL, PANEL), BF16),
            pltpu.VMEM((1536, 2 * COMPS + 128), BF16),
        ],
        compiler_params=MIDDLE,
        cost_estimate=pl.CostEstimate(flops=4 << 30, bytes_accessed=4 << 20, transcendentals=0),
    )(at, *pieces, comps, soon, *state)


def gram_kernel(at, *refs):
    own, recv, row_means, out = refs[:3], refs[3:6], refs[6], refs[7]
    rows, cols, stage, col_sums, sems, out_sems = refs[8:]
    fetch(at[0], own, recv, rows, cols, sems)
    copies = []
    for i in range(4):
        slot = i % 2
        if i >= 2:
            copies[i - 2].wait()
        span_i = slice(i * 256, (i + 1) * 256)
        row_mean = jnp.transpose(jnp.broadcast_to(row_means[:, span_i], (128, 256)))[:, :1]
        if i == 0:
            for m in range(4):
                fetched(own, rows, cols, sems, m)
                left = ones_beside(rows[m, :, :, :, :, span_i].reshape(512, 256))
                for j in range(8):
                    span = slice(j * 256, (j + 1) * 256)
                    right = cols[m, :, :, :, :, span].reshape(512, 256)
                    both = lax.dot_general(left, right, LEFT, preferred_element_type=F32)
                    tile, col_sum = both[:256], both[256:257]
                    if m > 0:
                        tile += stage[slot, :, span]
                        col_sum += col_sums[:, span]
                    if m == 3:
                        tile = (tile - row_mean * col_sum) * (1.0 / (SCANS - 1))
                    stage[slot, :, span] = tile
                    col_sums[:, span] = col_sum
        else:
            left = rows[:, :, :, :, :, span_i].reshape(SCANS, 256)
            for j in range(8):
                span = slice(j * 256, (j + 1) * 256)
                right = cols[:, :, :, :, :, span].reshape(SCANS, 256)
                tile = lax.dot_general(left, right, LEFT, preferred_element_type=F32)
                stage[slot, :, span] = (tile - row_mean * col_sums[:, span]) * (1.0 / (SCANS - 1))
        copy = pltpu.make_async_copy(stage.at[slot], out.at[pl.ds(i * 256, 256), :], out_sems.at[slot])
        copy.start()
        copies.append(copy)
    for copy in copies[2:]:
        copy.wait()


def gram(at, own, recv, row_means):
    return pl.pallas_call(
        gram_kernel,
        out_shape=jax.ShapeDtypeStruct((HALF, PANEL), F32),
        in_specs=[IN_SMEM] + [ANY] * 6 + [IN_VMEM],
        out_specs=ANY,
        scratch_shapes=[
            ROWS,
            COLS,
            pltpu.VMEM((2, 256, PANEL), F32),
            pltpu.VMEM((1, PANEL), F32),
            pltpu.SemaphoreType.DMA((4,)),
            pltpu.SemaphoreType.DMA((2,)),
        ],
        compiler_params=pltpu.CompilerParams(vmem_limit_bytes=30 << 20),
        cost_estimate=pl.CostEstimate(flops=8 << 30, bytes_accessed=20 << 20, transcendentals=0),
    )(at, *[pltpu.with_memory_space_constraint(piece, pltpu.HBM) for piece in own + recv], row_means)


def on_device(patterns, components):
    row = lax.axis_index("brow")
    col = lax.axis_index("bcol")
    k, y, xh = row % 2, (row // 2) % 4, row // 8
    z, xl = col % 4, col // 4
    first = k == 0
    same = jnp.where(first, y, z)
    at = jnp.stack([(same + d) % 4 for d in STEPS]).astype(jnp.int32)
    sends = pick(at, patterns, permute(patterns, swap))
    got = [sends[0]] + [permute(sends[n], spread(STEPS[n])) for n in range(1, 4)]
    own_half = jnp.where(first, xh, xl)
    at = jnp.stack(
        [own_half, jnp.where(first, own_half, 1 - own_half), jnp.where(first, 1 - own_half, own_half), 1 - own_half]
    ).astype(jnp.int32)
    group_own, to_1, to_2, to_3 = group(at, got)
    high = lax.reduce_precision(components, 8, 7)
    comps = jnp.concatenate([high, components - high], axis=1).astype(BF16)
    near = [permute(to_1, across(1)), permute(to_3, across(3))]
    ring_own = [permute(group_own, around(d)) for d in STEPS[1:]]
    near, to_2, comps = lax.optimization_barrier((near, to_2, comps))
    ring_own, near[0] = lax.optimization_barrier((ring_own, near[0]))
    far = permute(to_2, across(2))
    at = jnp.reshape(k, (1,)).astype(jnp.int32)
    own = jnp.stack([group_own] + ring_own)
    recv = permute(own, swap)
    group_near = jnp.stack(near)
    ring_near = [permute(group_near, around(d)) for d in STEPS[1:3]]
    state = own_part(at, own, recv, comps)
    far, ring_near, state = lax.optimization_barrier((far, ring_near, state))
    late = [permute(jnp.stack([ring_near[n][n], far]), around(STEPS[n + 1])) for n in range(2)]
    late.append(permute(far[None], around(STEPS[3])))
    own_soon = jnp.concatenate([group_near] + ring_near + [far[None]])
    recv_soon = permute(own_soon, swap)
    soon = soon_part(at, own_soon, recv_soon, comps)
    late, soon = lax.optimization_barrier((late, soon))
    own_late = jnp.concatenate(late)
    recv_late = permute(own_late, swap)
    parts, row_means = last_part(at, (own_soon, recv_soon, own_late, recv_late), comps, soon, state)
    own = [own, own_soon, own_late]
    recv = [recv, recv_soon, recv_late]
    parts = lax.all_to_all(parts, "bcol", 0, 0, tiled=True)
    covariance = gram(at, own, recv, row_means)
    projected = jnp.sum(parts, axis=0).T
    means_part = lax.dynamic_slice_in_dim(row_means[0], col * 128, 128, 0)
    return covariance, projected, means_part


def solution(mesh):
    return jax.shard_map(
        on_device,
        mesh=mesh,
        in_specs=(P(("brow", "bcol"), None), P("bcol", None)),
        out_specs=(P("brow", "bcol"), P(("brow", "bcol"), None), P(("brow", "bcol"))),
        check_vma=False,
    )
```

```python
import functools

import jax
import jax.numpy as jnp
from jax import lax
from jax.experimental import pallas as pl
from jax.experimental.pallas import tpu as pltpu
from jax.sharding import PartitionSpec as P

F32 = jnp.float32
BF16 = jnp.bfloat16
AXES = ("brow", "bcol")
SCANS = 2048
PIXELS = 16384
COMPS = 256
LOCAL = 16
PANEL = 2048
HALF = 1024
STEPS = (0, 1, -1, 2)
ANY = pl.BlockSpec(memory_space=pl.ANY)
IN_VMEM = pl.BlockSpec(memory_space=pltpu.VMEM)
IN_SMEM = pl.BlockSpec(memory_space=pltpu.SMEM)
MIDDLE = pltpu.CompilerParams(vmem_limit_bytes=24 << 20)
SMALL = pltpu.CompilerParams(vmem_limit_bytes=8 << 20)


def flat(x, y, z, k):
    return (((x // 2) * 4 + y) * 2 + k) * 8 + (x % 2) * 4 + z


def permute(value, move):
    pairs = []
    for x in range(4):
        for y in range(4):
            for z in range(4):
                for k in range(2):
                    x2, y2, z2, k2 = move(x, y, z, k)
                    pairs.append((flat(x, y, z, k), flat(x2, y2 % 4, z2 % 4, k2)))
    return lax.ppermute(value, AXES, pairs)


def spread(d):
    return lambda x, y, z, k: (x, y + d, z, k) if k == 0 else (x, y, z + d, k)


def across(m):
    return lambda x, y, z, k: (x ^ m, y, z, k)


def around(d):
    return lambda x, y, z, k: (x, y, z + d, k) if k == 0 else (x, y + d, z, k)


def swap(x, y, z, k):
    return x, y, z, 1 - k


def pick_kernel(at, mine, other, *refs):
    pieces, sems = refs[:4], refs[4]
    copies = []
    for n, piece in enumerate(pieces):
        for half in range(2):
            span = pl.ds(pl.multiple_of((half * 4 + at[n]) * PANEL, PANEL), PANEL)
            copies.append(pltpu.make_async_copy(mine.at[:, span], piece.at[half, 0], sems.at[2 * n + half]))
            copies[-1].start()
    for n, piece in enumerate(pieces):
        for half in range(2):
            span = pl.ds(pl.multiple_of((half * 4 + at[n]) * PANEL, PANEL), PANEL)
            piece[half, 1] = other[:, span]
    for copy in copies:
        copy.wait()


def pick(at, mine, other):
    return pl.pallas_call(
        pick_kernel,
        out_shape=[jax.ShapeDtypeStruct((2, 2, LOCAL, PANEL), BF16)] * 4,
        in_specs=[IN_SMEM, ANY, IN_VMEM],
        out_specs=[IN_VMEM] * 4,
        scratch_shapes=[pltpu.SemaphoreType.DMA((8,))],
        compiler_params=SMALL,
    )(at, mine, other)


def group_kernel(at, *refs):
    pieces, groups = refs[:4], refs[4:]
    for n, group in enumerate(groups):
        for i, piece in enumerate(pieces):
            for source in range(2):
                group[source, i] = piece[at[n], source]


def group(at, pieces):
    return pl.pallas_call(
        group_kernel,
        out_shape=[jax.ShapeDtypeStruct((2, 4, LOCAL, PANEL), BF16)] * 4,
        in_specs=[IN_SMEM] + [IN_VMEM] * 4,
        out_specs=[IN_VMEM] * 4,
        compiler_params=SMALL,
    )(at, *pieces)


def pack_kernel(plan, *refs):
    sources, packed = refs[: -len(plan)], refs[-len(plan) :]
    for out, parts in zip(packed, plan):
        at = 0
        for n, first, last in parts:
            out[at : at + last - first] = sources[n][first:last]
            at += last - first


def pack(plan, *sources):
    sizes = [sum(last - first for _, first, last in parts) for parts in plan]
    return pl.pallas_call(
        functools.partial(pack_kernel, plan),
        out_shape=[jax.ShapeDtypeStruct((size, 4, LOCAL, PANEL), BF16) for size in sizes],
        in_specs=[IN_VMEM] * len(sources),
        out_specs=[IN_VMEM] * len(sizes),
        compiler_params=SMALL,
    )(*sources)


EARLY = [(0, 0), (0, 1), (0, 2), (1, 0), (2, 0)]
SOON = [(0, 3), (1, 1), (2, 1), (1, 2), (2, 2), (3, 0)]
LATE = [(1, 3), (3, 1), (2, 3), (3, 2), (3, 3)]
ORDER = (EARLY, SOON, LATE)
WIDTH = 128
LEFT = (((0,), (0,)), ((), ()))


def fetch(core, own, recv, rows, cols, sems):
    def start(row_from, col_from, offset):
        for row, col, labels in zip(row_from, col_from, ORDER):
            for i, (m, step) in enumerate(labels):
                pltpu.make_async_copy(col.at[i], cols.at[m, step], sems.at[m]).start()
                for s in range(2):
                    pltpu.make_async_copy(
                        row.at[i, s, :, :, pl.ds(offset, HALF)], rows.at[m, :, 1 - s, step], sems.at[m]
                    ).start()

    @pl.when(core == 0)
    def _():
        start(own, recv, 0)

    @pl.when(core == 1)
    def _():
        start(recv, own, HALF)


def fetched(own, rows, cols, sems, which):
    for array, labels in zip(own, ORDER):
        for i, (m, step) in enumerate(labels):
            if m == which:
                pltpu.make_async_copy(array.at[i], cols.at[m, step], sems.at[m]).wait()
                for s in range(2):
                    pltpu.make_async_copy(
                        array.at[i, s, :, :, pl.ds(0, HALF)], rows.at[m, :, 1 - s, step], sems.at[m]
                    ).wait()


ROWS = pltpu.VMEM((4, 4, 2, 4, LOCAL, HALF), BF16)
COLS = pltpu.VMEM((4, 4, 2, 4, LOCAL, PANEL), BF16)


def ones_beside(block):
    return jnp.concatenate([block, jnp.ones((block.shape[0], 128), BF16)], axis=1)


def score_of(comps, block):
    score = jnp.dot(block, comps, preferred_element_type=F32)
    return (score[:, :COMPS] + score[:, COMPS:]).T


def left_of(centred):
    high = centred.astype(BF16)
    low = (centred - high.astype(F32)).astype(BF16)
    return jnp.concatenate([high, low, jnp.ones((16, centred.shape[1]), BF16)], axis=0)


def product_of(left, panel):
    product = jnp.dot(left, panel, preferred_element_type=F32)
    return product[:COMPS] + product[COMPS : 2 * COMPS], product[2 * COMPS : 2 * COMPS + 1]


def select(core, own, recv, use):
    @pl.when(core == 0)
    def _():
        use(own, recv, 0)

    @pl.when(core == 1)
    def _():
        use(recv, own, HALF)


def early_kernel(at, own, recv, components, scores, origin, comps, cols):
    comps[:, :COMPS] = components[...].astype(BF16)
    comps[:, COMPS:] = (components[...] - comps[:, :COMPS].astype(F32)).astype(BF16)

    def use(row_from, col_from, offset):
        cols[...] = col_from[...]

    select(at[0], own, recv, use)
    score = score_of(comps[...], cols[...].reshape(len(EARLY) * WIDTH, PANEL))
    scores[...] = score
    mean = jnp.sum(score, axis=1, keepdims=True) * (1.0 / score.shape[1])
    origin[...] = jnp.broadcast_to(mean, (COMPS, 128))


def early_part(at, own, recv, comps):
    return pl.pallas_call(
        early_kernel,
        out_shape=[
            jax.ShapeDtypeStruct((COMPS, len(EARLY) * WIDTH), F32),
            jax.ShapeDtypeStruct((COMPS, 128), F32),
            jax.ShapeDtypeStruct((PANEL, 2 * COMPS), BF16),
        ],
        in_specs=[IN_SMEM] + [IN_VMEM] * 3,
        out_specs=[IN_VMEM] * 3,
        scratch_shapes=[pltpu.VMEM((len(EARLY), 2, 4, LOCAL, PANEL), BF16)],
        compiler_params=MIDDLE,
        cost_estimate=pl.CostEstimate(flops=1 << 30, bytes_accessed=1 << 20, transcendentals=0),
    )(at, own, recv, comps)


def fill_rows(rows, groups, pieces, offset):
    for n, m in enumerate(groups):
        for step in range(4):
            array, i = pieces(m, step)
            for s in range(2):
                rows[n, :, 1 - s, step] = array[i, s, :, :, offset : offset + HALF]


def find(arrays, m, step):
    for array, labels in zip(arrays, ORDER):
        if (m, step) in labels:
            return array, labels.index((m, step))


def soon_kernel(at, *refs):
    own, recv, comps, early, origin, scores, total, row_sum, rows, cols = refs[:2], refs[2:4], *refs[4:]

    def use(row_from, col_from, offset):
        cols[...] = col_from[1][...]
        fill_rows(rows, (0,), lambda m, step: find(row_from, m, step), offset)

    select(at[0], own, recv, use)
    score = score_of(comps[...], cols[...].reshape(len(SOON) * WIDTH, PANEL))
    scores[...] = score
    first = jnp.concatenate([early[:, : 3 * WIDTH], score[:, :WIDTH]], axis=1)
    total[...], row_sum[...] = product_of(left_of(first - origin[:, :1]), rows[...].reshape(4 * WIDTH, HALF))


def soon_part(at, own, recv, comps, early):
    return pl.pallas_call(
        soon_kernel,
        out_shape=[
            jax.ShapeDtypeStruct((COMPS, len(SOON) * WIDTH), F32),
            jax.ShapeDtypeStruct((COMPS, HALF), F32),
            jax.ShapeDtypeStruct((1, HALF), F32),
        ],
        in_specs=[IN_SMEM] + [IN_VMEM] * 7,
        out_specs=[IN_VMEM] * 3,
        scratch_shapes=[
            pltpu.VMEM((1, 4, 2, 4, LOCAL, HALF), BF16),
            pltpu.VMEM((len(SOON), 2, 4, LOCAL, PANEL), BF16),
        ],
        compiler_params=MIDDLE,
        cost_estimate=pl.CostEstimate(flops=2 << 30, bytes_accessed=1 << 20, transcendentals=0),
    )(at, *own, *recv, comps, *early)


def late_kernel(own, comps, scores):
    scores[...] = score_of(comps[...], own[...].reshape(len(LATE) * WIDTH, PANEL))


def late_part(own, comps):
    return pl.pallas_call(
        late_kernel,
        out_shape=jax.ShapeDtypeStruct((COMPS, len(LATE) * WIDTH), F32),
        in_specs=[IN_VMEM] * 2,
        out_specs=IN_VMEM,
        compiler_params=SMALL,
        cost_estimate=pl.CostEstimate(flops=1 << 30, bytes_accessed=1 << 20, transcendentals=0),
    )(own, comps)


def last_kernel(at, *refs):
    own, recv, early, origin, soon, total_in, rs_in, late_own, late_recv = refs[:3], refs[3:6], *refs[6:13]
    parts, means, rows, left = refs[13:]

    def put(block, labels):
        for i, (m, step) in enumerate(labels):
            if m > 0:
                at_scan = ((m - 1) * 4 + step) * WIDTH
                left[:, at_scan : at_scan + WIDTH] = left_of(block[:, i * WIDTH : (i + 1) * WIDTH] - origin[:, :1])

    def use(row_from, col_from, offset):
        fill_rows(rows, (1, 2, 3), lambda m, step: find(row_from, m, step), offset)
        put(late_recv if offset == 0 else late_own, LATE)

    select(at[0], own, recv, use)
    put(early, EARLY)
    put(soon, SOON)
    late = jnp.where(at[0] == 0, late_recv[...], late_own[...])
    score_sum = sum(jnp.sum(block, axis=1, keepdims=True) for block in (early[...], soon[...], late))
    total, row_sum = product_of(left[...], rows[...].reshape(12 * WIDTH, HALF))
    row_sum = row_sum + rs_in[...]
    shift = score_sum * (1.0 / SCANS) - origin[:, :1]
    total = (total + total_in[...] - shift * row_sum) * (1.0 / (SCANS - 1))
    for c in range(8):
        parts[c] = total[:, c * 128 : (c + 1) * 128]
    means[...] = row_sum * (1.0 / SCANS)


def last_part(at, own, recv, state):
    return pl.pallas_call(
        last_kernel,
        out_shape=[jax.ShapeDtypeStruct((8, COMPS, 128), F32), jax.ShapeDtypeStruct((1, HALF), F32)],
        in_specs=[IN_SMEM] + [IN_VMEM] * 13,
        out_specs=[IN_VMEM] * 2,
        scratch_shapes=[
            pltpu.VMEM((3, 4, 2, 4, LOCAL, HALF), BF16),
            pltpu.VMEM((2 * COMPS + 16, 12 * WIDTH), BF16),
        ],
        compiler_params=MIDDLE,
        cost_estimate=pl.CostEstimate(flops=4 << 30, bytes_accessed=4 << 20, transcendentals=0),
    )(at, *own, *recv, *state)


def gram_kernel(at, *refs):
    own, recv, row_means, out = refs[:3], refs[3:6], refs[6], refs[7]
    rows, cols, stage, col_sums, sems, out_sems = refs[8:]
    fetch(at[0], own, recv, rows, cols, sems)
    copies = []
    for i in range(4):
        slot = i % 2
        if i >= 2:
            copies[i - 2].wait()
        span_i = slice(i * 256, (i + 1) * 256)
        row_mean = jnp.transpose(jnp.broadcast_to(row_means[:, span_i], (128, 256)))[:, :1]
        if i == 0:
            for m in range(4):
                fetched(own, rows, cols, sems, m)
                left = ones_beside(rows[m, :, :, :, :, span_i].reshape(512, 256))
                for j in range(8):
                    span = slice(j * 256, (j + 1) * 256)
                    right = cols[m, :, :, :, :, span].reshape(512, 256)
                    both = lax.dot_general(left, right, LEFT, preferred_element_type=F32)
                    tile, col_sum = both[:256], both[256:257]
                    if m > 0:
                        tile += stage[slot, :, span]
                        col_sum += col_sums[:, span]
                    if m == 3:
                        tile = (tile - row_mean * col_sum) * (1.0 / (SCANS - 1))
                    stage[slot, :, span] = tile
                    col_sums[:, span] = col_sum
        else:
            left = rows[:, :, :, :, :, span_i].reshape(SCANS, 256)
            for j in range(8):
                span = slice(j * 256, (j + 1) * 256)
                right = cols[:, :, :, :, :, span].reshape(SCANS, 256)
                tile = lax.dot_general(left, right, LEFT, preferred_element_type=F32)
                stage[slot, :, span] = (tile - row_mean * col_sums[:, span]) * (1.0 / (SCANS - 1))
        copy = pltpu.make_async_copy(stage.at[slot], out.at[pl.ds(i * 256, 256), :], out_sems.at[slot])
        copy.start()
        copies.append(copy)
    for copy in copies[2:]:
        copy.wait()


def gram(at, own, recv, row_means):
    return pl.pallas_call(
        gram_kernel,
        out_shape=jax.ShapeDtypeStruct((HALF, PANEL), F32),
        in_specs=[IN_SMEM] + [ANY] * 6 + [IN_VMEM],
        out_specs=ANY,
        scratch_shapes=[
            ROWS,
            COLS,
            pltpu.VMEM((2, 256, PANEL), F32),
            pltpu.VMEM((1, PANEL), F32),
            pltpu.SemaphoreType.DMA((4,)),
            pltpu.SemaphoreType.DMA((2,)),
        ],
        compiler_params=pltpu.CompilerParams(vmem_limit_bytes=30 << 20),
        cost_estimate=pl.CostEstimate(flops=8 << 30, bytes_accessed=20 << 20, transcendentals=0),
    )(at, *[pltpu.with_memory_space_constraint(piece, pltpu.HBM) for piece in own + recv], row_means)


def on_device(patterns, components):
    row = lax.axis_index("brow")
    col = lax.axis_index("bcol")
    k, y, xh = row % 2, (row // 2) % 4, row // 8
    z, xl = col % 4, col // 4
    first = k == 0
    same = jnp.where(first, y, z)
    at = jnp.stack([(same + d) % 4 for d in STEPS]).astype(jnp.int32)
    sends = pick(at, patterns, permute(patterns, swap))
    got = [sends[0]] + [permute(sends[n], spread(STEPS[n])) for n in range(1, 4)]
    own_half = jnp.where(first, xh, xl)
    at = jnp.stack(
        [own_half, jnp.where(first, own_half, 1 - own_half), jnp.where(first, 1 - own_half, own_half), 1 - own_half]
    ).astype(jnp.int32)
    group_own, to_1, to_2, to_3 = group(at, got)
    at = jnp.reshape(k, (1,)).astype(jnp.int32)
    near = [permute(to_1, across(1)), permute(to_3, across(3))]
    ring_own = [permute(group_own, around(d)) for d in STEPS[1:3]]
    near, ring_own, to_2 = lax.optimization_barrier((near, ring_own, to_2))
    far = permute(to_2, across(2))
    ring = pack((((0, 0, 2), (1, 0, 2), (2, 0, 1)), ((0, 0, 2), (1, 0, 2), (3, 1, 2))), *near, *ring_own)
    ring = [permute(ring[n], around(STEPS[n + 1])) for n in range(2)]
    (own_early,) = pack((tuple((n, 0, 2) for n in range(5)),), group_own, *ring_own, *near)
    own_early = own_early.reshape((5, 2, 4, LOCAL, PANEL))
    recv_early = permute(own_early, swap)
    *early, comps = early_part(at, own_early, recv_early, components)
    far, ring, early = lax.optimization_barrier((far, ring, early))
    late = pack((((0, 0, 2), (2, 0, 2)), ((1, 2, 4), (2, 0, 2))), *ring, far)
    late = [permute(late[n], around(STEPS[n + 1])) for n in range(2)]
    late.append(permute(far, around(STEPS[3])))
    (own_soon,) = pack((((0, 4, 5), (1, 4, 5), (0, 0, 4), (1, 0, 4), (2, 0, 2)),), *ring, far)
    own_soon = own_soon.reshape((6, 2, 4, LOCAL, PANEL))
    recv_soon = permute(own_soon, swap)
    soon = soon_part(at, (own_early, own_soon), (recv_early, recv_soon), comps, early)
    late, soon = lax.optimization_barrier((late, soon))
    (own_late,) = pack((((0, 0, 4), (1, 0, 4), (2, 0, 2)),), *late)
    own_late = own_late.reshape((5, 2, 4, LOCAL, PANEL))
    recv_late = permute(own_late, swap)
    own = [own_early, own_soon, own_late]
    recv = [recv_early, recv_soon, recv_late]
    scores = late_part(own_late, comps)
    parts, row_means = last_part(at, own, recv, (*early, *soon, scores, permute(scores, swap)))
    parts = lax.all_to_all(parts, "bcol", 0, 0, tiled=True)
    covariance = gram(at, own, recv, row_means)
    projected = jnp.sum(parts, axis=0).T
    means_part = lax.dynamic_slice_in_dim(row_means[0], col * 128, 128, 0)
    return covariance, projected, means_part


def solution(mesh):
    return jax.shard_map(
        on_device,
        mesh=mesh,
        in_specs=(P(("brow", "bcol"), None), P("bcol", None)),
        out_specs=(P("brow", "bcol"), P(("brow", "bcol"), None), P(("brow", "bcol"))),
        check_vma=False,
    )
```

```python
import functools

import jax
import jax.numpy as jnp
from jax import lax
from jax.experimental import pallas as pl
from jax.experimental.pallas import tpu as pltpu
from jax.sharding import PartitionSpec as P

F32 = jnp.float32
BF16 = jnp.bfloat16
AXES = ("brow", "bcol")
SCANS = 2048
PIXELS = 16384
COMPS = 256
LOCAL = 16
PANEL = 2048
HALF = 1024
STEPS = (0, 1, -1, 2)
ANY = pl.BlockSpec(memory_space=pl.ANY)
IN_VMEM = pl.BlockSpec(memory_space=pltpu.VMEM)
IN_SMEM = pl.BlockSpec(memory_space=pltpu.SMEM)
MIDDLE = pltpu.CompilerParams(vmem_limit_bytes=24 << 20)
SMALL = pltpu.CompilerParams(vmem_limit_bytes=8 << 20)


def flat(x, y, z, k):
    return (((x // 2) * 4 + y) * 2 + k) * 8 + (x % 2) * 4 + z


def permute(value, move):
    pairs = []
    for x in range(4):
        for y in range(4):
            for z in range(4):
                for k in range(2):
                    x2, y2, z2, k2 = move(x, y, z, k)
                    pairs.append((flat(x, y, z, k), flat(x2, y2 % 4, z2 % 4, k2)))
    return lax.ppermute(value, AXES, pairs)


def spread(d):
    return lambda x, y, z, k: (x, y + d, z, k) if k == 0 else (x, y, z + d, k)


def across(m):
    return lambda x, y, z, k: (x ^ m, y, z, k)


def around(d):
    return lambda x, y, z, k: (x, y, z + d, k) if k == 0 else (x, y + d, z, k)


def swap(x, y, z, k):
    return x, y, z, 1 - k


def span_of(place, n, half):
    start = (half * 4 + lax.rem(place[0] + STEPS[n] + 4, 4)) * PANEL
    return pl.ds(pl.multiple_of(start, PANEL), PANEL)


def pick_kernel(place, mine, *refs):
    pieces, sems = refs[:4], refs[4]
    copies = []
    for n, piece in enumerate(pieces):
        for half in range(2):
            span = span_of(place, n, half)
            copies.append(pltpu.make_async_copy(mine.at[:, span], piece.at[half], sems.at[2 * n + half]))
            copies[-1].start()
    for copy in copies:
        copy.wait()


def pick(at, mine):
    return pl.pallas_call(
        pick_kernel,
        out_shape=[jax.ShapeDtypeStruct((2, LOCAL, PANEL), BF16)] * 4,
        in_specs=[IN_SMEM, ANY],
        out_specs=[IN_VMEM] * 4,
        scratch_shapes=[pltpu.SemaphoreType.DMA((8,))],
        compiler_params=SMALL,
    )(at, mine)


def join_kernel(place, other, *refs):
    for n, (mine, piece) in enumerate(zip(refs[:4], refs[4:])):
        for half in range(2):
            span = span_of(place, n, half)
            piece[half, 0] = mine[half]
            piece[half, 1] = other[:, span]


def join(at, other, mine):
    return pl.pallas_call(
        join_kernel,
        out_shape=[jax.ShapeDtypeStruct((2, 2, LOCAL, PANEL), BF16)] * 4,
        in_specs=[IN_SMEM] + [IN_VMEM] * 5,
        out_specs=[IN_VMEM] * 4,
        compiler_params=SMALL,
    )(at, other, *mine)


def group_kernel(core, own_half, *refs):
    pieces, groups = refs[:4], refs[4:]
    half = own_half[0]
    crossed = half + core[0] - 2 * half * core[0]
    for group, choice in zip(groups, (half, crossed, 1 - crossed, 1 - half)):
        for i, piece in enumerate(pieces):
            for source in range(2):
                group[source, i] = piece[choice, source]


def group(core, own_half, pieces):
    return pl.pallas_call(
        group_kernel,
        out_shape=[jax.ShapeDtypeStruct((2, 4, LOCAL, PANEL), BF16)] * 4,
        in_specs=[IN_SMEM] * 2 + [IN_VMEM] * 4,
        out_specs=[IN_VMEM] * 4,
        compiler_params=SMALL,
    )(core, own_half, *pieces)


def pack_kernel(plan, *refs):
    sources, packed = refs[: -len(plan)], refs[-len(plan) :]
    for out, parts in zip(packed, plan):
        at = 0
        for n, first, last in parts:
            out[at : at + last - first] = sources[n][first:last]
            at += last - first


def pack(plan, *sources):
    sizes = [sum(last - first for _, first, last in parts) for parts in plan]
    return pl.pallas_call(
        functools.partial(pack_kernel, plan),
        out_shape=[jax.ShapeDtypeStruct((size, 4, LOCAL, PANEL), BF16) for size in sizes],
        in_specs=[IN_VMEM] * len(sources),
        out_specs=[IN_VMEM] * len(sizes),
        compiler_params=SMALL,
    )(*sources)


EARLY = [(0, 0), (0, 1), (0, 2), (1, 0), (2, 0)]
SOON = [(0, 3), (1, 1), (2, 1), (1, 2), (2, 2), (3, 0)]
LATE = [(1, 3), (3, 1), (2, 3), (3, 2), (3, 3)]
ORDER = (EARLY, SOON, LATE)
WIDTH = 128
LEFT = (((0,), (0,)), ((), ()))


def fetch(core, own, recv, rows, cols, sems):
    def start(row_from, col_from, offset):
        for row, col, labels in zip(row_from, col_from, ORDER):
            for i, (m, step) in enumerate(labels):
                pltpu.make_async_copy(col.at[i], cols.at[m, step], sems.at[m]).start()
                for s in range(2):
                    pltpu.make_async_copy(
                        row.at[i, s, :, :, pl.ds(offset, HALF)], rows.at[m, :, 1 - s, step], sems.at[m]
                    ).start()

    @pl.when(core == 0)
    def _():
        start(own, recv, 0)

    @pl.when(core == 1)
    def _():
        start(recv, own, HALF)


def fetched(own, rows, cols, sems, which):
    for array, labels in zip(own, ORDER):
        for i, (m, step) in enumerate(labels):
            if m == which:
                pltpu.make_async_copy(array.at[i], cols.at[m, step], sems.at[m]).wait()
                for s in range(2):
                    pltpu.make_async_copy(
                        array.at[i, s, :, :, pl.ds(0, HALF)], rows.at[m, :, 1 - s, step], sems.at[m]
                    ).wait()


ROWS = pltpu.VMEM((4, 4, 2, 4, LOCAL, HALF), BF16)
COLS = pltpu.VMEM((4, 4, 2, 4, LOCAL, PANEL), BF16)


def ones_beside(block):
    return jnp.concatenate([block, jnp.ones((block.shape[0], 128), BF16)], axis=1)


def score_of(comps, block):
    score = jnp.dot(block, comps, preferred_element_type=F32)
    return (score[:, :COMPS] + score[:, COMPS:]).T


def left_of(centred):
    high = centred.astype(BF16)
    low = (centred - high.astype(F32)).astype(BF16)
    return jnp.concatenate([high, low, jnp.ones((16, centred.shape[1]), BF16)], axis=0)


def product_of(left, panel):
    product = jnp.dot(left, panel, preferred_element_type=F32)
    return product[:COMPS] + product[COMPS : 2 * COMPS], product[2 * COMPS : 2 * COMPS + 1]


def select(core, own, recv, use):
    @pl.when(core == 0)
    def _():
        use(own, recv, 0)

    @pl.when(core == 1)
    def _():
        use(recv, own, HALF)


def early_kernel(at, own, recv, components, scores, origin, comps, cols):
    comps[:, :COMPS] = components[...].astype(BF16)
    comps[:, COMPS:] = (components[...] - comps[:, :COMPS].astype(F32)).astype(BF16)

    def use(row_from, col_from, offset):
        cols[...] = col_from[...]

    select(at[0], own, recv, use)
    score = score_of(comps[...], cols[...].reshape(len(EARLY) * WIDTH, PANEL))
    scores[...] = score
    mean = jnp.sum(score, axis=1, keepdims=True) * (1.0 / score.shape[1])
    origin[...] = jnp.broadcast_to(mean, (COMPS, 128))


def early_part(at, own, recv, comps):
    return pl.pallas_call(
        early_kernel,
        out_shape=[
            jax.ShapeDtypeStruct((COMPS, len(EARLY) * WIDTH), F32),
            jax.ShapeDtypeStruct((COMPS, 128), F32),
            jax.ShapeDtypeStruct((PANEL, 2 * COMPS), BF16),
        ],
        in_specs=[IN_SMEM] + [IN_VMEM] * 3,
        out_specs=[IN_VMEM] * 3,
        scratch_shapes=[pltpu.VMEM((len(EARLY), 2, 4, LOCAL, PANEL), BF16)],
        compiler_params=MIDDLE,
        cost_estimate=pl.CostEstimate(flops=1 << 30, bytes_accessed=1 << 20, transcendentals=0),
    )(at, own, recv, comps)


def fill_rows(rows, groups, pieces, offset):
    for n, m in enumerate(groups):
        for step in range(4):
            array, i = pieces(m, step)
            for s in range(2):
                rows[n, :, 1 - s, step] = array[i, s, :, :, offset : offset + HALF]


def find(arrays, m, step):
    for array, labels in zip(arrays, ORDER):
        if (m, step) in labels:
            return array, labels.index((m, step))


def soon_kernel(at, *refs):
    own, recv, comps, early, origin, scores, total, row_sum, rows, cols = refs[:2], refs[2:4], *refs[4:]

    def use(row_from, col_from, offset):
        cols[...] = col_from[1][...]
        fill_rows(rows, (0,), lambda m, step: find(row_from, m, step), offset)

    select(at[0], own, recv, use)
    score = score_of(comps[...], cols[...].reshape(len(SOON) * WIDTH, PANEL))
    scores[...] = score
    first = jnp.concatenate([early[:, : 3 * WIDTH], score[:, :WIDTH]], axis=1)
    total[...], row_sum[...] = product_of(left_of(first - origin[:, :1]), rows[...].reshape(4 * WIDTH, HALF))


def soon_part(at, own, recv, comps, early):
    return pl.pallas_call(
        soon_kernel,
        out_shape=[
            jax.ShapeDtypeStruct((COMPS, len(SOON) * WIDTH), F32),
            jax.ShapeDtypeStruct((COMPS, HALF), F32),
            jax.ShapeDtypeStruct((1, HALF), F32),
        ],
        in_specs=[IN_SMEM] + [IN_VMEM] * 7,
        out_specs=[IN_VMEM] * 3,
        scratch_shapes=[
            pltpu.VMEM((1, 4, 2, 4, LOCAL, HALF), BF16),
            pltpu.VMEM((len(SOON), 2, 4, LOCAL, PANEL), BF16),
        ],
        compiler_params=MIDDLE,
        cost_estimate=pl.CostEstimate(flops=2 << 30, bytes_accessed=1 << 20, transcendentals=0),
    )(at, *own, *recv, comps, *early)


def late_kernel(own, comps, scores):
    scores[...] = score_of(comps[...], own[...].reshape(len(LATE) * WIDTH, PANEL))


def late_part(own, comps):
    return pl.pallas_call(
        late_kernel,
        out_shape=jax.ShapeDtypeStruct((COMPS, len(LATE) * WIDTH), F32),
        in_specs=[IN_VMEM] * 2,
        out_specs=IN_VMEM,
        compiler_params=SMALL,
        cost_estimate=pl.CostEstimate(flops=1 << 30, bytes_accessed=1 << 20, transcendentals=0),
    )(own, comps)


def last_kernel(at, column, *refs):
    own, recv, early, origin, soon, total_in, rs_in, late_own, late_recv = refs[:3], refs[3:6], *refs[6:13]
    parts, means, means_part, rows, left = refs[13:]

    def put(block, labels):
        for i, (m, step) in enumerate(labels):
            if m > 0:
                at_scan = ((m - 1) * 4 + step) * WIDTH
                left[:, at_scan : at_scan + WIDTH] = left_of(block[:, i * WIDTH : (i + 1) * WIDTH] - origin[:, :1])

    def use(row_from, col_from, offset):
        fill_rows(rows, (1, 2, 3), lambda m, step: find(row_from, m, step), offset)
        put(late_recv if offset == 0 else late_own, LATE)

    select(at[0], own, recv, use)
    put(early, EARLY)
    put(soon, SOON)
    late = jnp.where(at[0] == 0, late_recv[...], late_own[...])
    score_sum = sum(jnp.sum(block, axis=1, keepdims=True) for block in (early[...], soon[...], late))
    total, row_sum = product_of(left[...], rows[...].reshape(12 * WIDTH, HALF))
    row_sum = row_sum + rs_in[...]
    shift = score_sum * (1.0 / SCANS) - origin[:, :1]
    total = (total + total_in[...] - shift * row_sum) * (1.0 / (SCANS - 1))
    for c in range(8):
        parts[c] = total[:, c * 128 : (c + 1) * 128]
    means[...] = row_sum * (1.0 / SCANS)
    means_part[...] = means[:, pl.ds(pl.multiple_of(column[0] * 128, 128), 128)]


def last_part(at, column, own, recv, state):
    return pl.pallas_call(
        last_kernel,
        out_shape=[
            jax.ShapeDtypeStruct((8, COMPS, 128), F32),
            jax.ShapeDtypeStruct((1, HALF), F32),
            jax.ShapeDtypeStruct((1, 128), F32),
        ],
        in_specs=[IN_SMEM] * 2 + [IN_VMEM] * 13,
        out_specs=[IN_VMEM] * 3,
        scratch_shapes=[
            pltpu.VMEM((3, 4, 2, 4, LOCAL, HALF), BF16),
            pltpu.VMEM((2 * COMPS + 16, 12 * WIDTH), BF16),
        ],
        compiler_params=MIDDLE,
        cost_estimate=pl.CostEstimate(flops=4 << 30, bytes_accessed=4 << 20, transcendentals=0),
    )(at, column, *own, *recv, *state)


def gram_kernel(at, *refs):
    own, recv, row_means, out = refs[:3], refs[3:6], refs[6], refs[7]
    rows, cols, stage, col_sums, sems, out_sems = refs[8:]
    fetch(at[0], own, recv, rows, cols, sems)
    copies = []
    for i in range(4):
        slot = i % 2
        if i >= 2:
            copies[i - 2].wait()
        span_i = slice(i * 256, (i + 1) * 256)
        row_mean = jnp.transpose(jnp.broadcast_to(row_means[:, span_i], (128, 256)))[:, :1]
        if i == 0:
            for m in range(4):
                fetched(own, rows, cols, sems, m)
                left = ones_beside(rows[m, :, :, :, :, span_i].reshape(512, 256))
                for j in range(8):
                    span = slice(j * 256, (j + 1) * 256)
                    right = cols[m, :, :, :, :, span].reshape(512, 256)
                    both = lax.dot_general(left, right, LEFT, preferred_element_type=F32)
                    tile, col_sum = both[:256], both[256:257]
                    if m > 0:
                        tile += stage[slot, :, span]
                        col_sum += col_sums[:, span]
                    if m == 3:
                        tile = (tile - row_mean * col_sum) * (1.0 / (SCANS - 1))
                    stage[slot, :, span] = tile
                    col_sums[:, span] = col_sum
        else:
            left = rows[:, :, :, :, :, span_i].reshape(SCANS, 256)
            for j in range(8):
                span = slice(j * 256, (j + 1) * 256)
                right = cols[:, :, :, :, :, span].reshape(SCANS, 256)
                tile = lax.dot_general(left, right, LEFT, preferred_element_type=F32)
                stage[slot, :, span] = (tile - row_mean * col_sums[:, span]) * (1.0 / (SCANS - 1))
        copy = pltpu.make_async_copy(stage.at[slot], out.at[pl.ds(i * 256, 256), :], out_sems.at[slot])
        copy.start()
        copies.append(copy)
    for copy in copies[2:]:
        copy.wait()


def gram(at, own, recv, row_means):
    return pl.pallas_call(
        gram_kernel,
        out_shape=jax.ShapeDtypeStruct((HALF, PANEL), F32),
        in_specs=[IN_SMEM] + [ANY] * 6 + [IN_VMEM],
        out_specs=ANY,
        scratch_shapes=[
            ROWS,
            COLS,
            pltpu.VMEM((2, 256, PANEL), F32),
            pltpu.VMEM((1, PANEL), F32),
            pltpu.SemaphoreType.DMA((4,)),
            pltpu.SemaphoreType.DMA((2,)),
        ],
        compiler_params=pltpu.CompilerParams(vmem_limit_bytes=30 << 20),
        cost_estimate=pl.CostEstimate(flops=8 << 30, bytes_accessed=20 << 20, transcendentals=0),
    )(at, *[pltpu.with_memory_space_constraint(piece, pltpu.HBM) for piece in own + recv], row_means)


def scalar(value):
    return jnp.reshape(value, (1,)).astype(jnp.int32)


def on_device(patterns, components):
    row = lax.axis_index("brow")
    col = lax.axis_index("bcol")
    k, y, xh = row % 2, (row // 2) % 4, row // 8
    z, xl = col % 4, col // 4
    first = k == 0
    same = jnp.where(first, y, z)
    at = scalar(same)
    mine = pick(at, pltpu.with_memory_space_constraint(patterns, pltpu.HBM))
    sends = join(at, permute(patterns, swap), mine)
    got = {n: permute(sends[n], spread(STEPS[n])) for n in (3, 1, 2)}
    got = [sends[0]] + [got[n] for n in range(1, 4)]
    own_half = jnp.where(first, xh, xl)
    group_own, to_1, to_2, to_3 = group(scalar(k), scalar(own_half), got)
    at = scalar(k)
    near = [permute(to_1, across(1)), permute(to_3, across(3))]
    ring_own = [permute(group_own, around(d)) for d in STEPS[1:3]]
    near, ring_own, to_2 = lax.optimization_barrier((near, ring_own, to_2))
    far = permute(to_2, across(2))
    ring = pack((((0, 0, 2), (1, 0, 2), (2, 0, 1)), ((0, 0, 2), (1, 0, 2), (3, 1, 2))), *near, *ring_own)
    ring = [permute(ring[n], around(STEPS[n + 1])) for n in range(2)]
    (own_early,) = pack((tuple((n, 0, 2) for n in range(5)),), group_own, *ring_own, *near)
    own_early = own_early.reshape((5, 2, 4, LOCAL, PANEL))
    recv_early = permute(own_early, swap)
    *early, comps = early_part(at, own_early, recv_early, components)
    far, ring, early = lax.optimization_barrier((far, ring, early))
    late = pack((((0, 0, 2), (2, 0, 2)), ((1, 2, 4), (2, 0, 2))), *ring, far)
    opposite = permute(far, around(STEPS[3]))
    late = [permute(late[n], around(STEPS[n + 1])) for n in range(2)] + [opposite]
    (own_soon,) = pack((((0, 4, 5), (1, 4, 5), (0, 0, 4), (1, 0, 4), (2, 0, 2)),), *ring, far)
    own_soon = own_soon.reshape((6, 2, 4, LOCAL, PANEL))
    recv_soon = permute(own_soon, swap)
    soon = soon_part(at, (own_early, own_soon), (recv_early, recv_soon), comps, early)
    late, soon = lax.optimization_barrier((late, soon))
    (own_late,) = pack((((0, 0, 4), (1, 0, 4), (2, 0, 2)),), *late)
    own_late = own_late.reshape((5, 2, 4, LOCAL, PANEL))
    recv_late = permute(own_late, swap)
    own = [own_early, own_soon, own_late]
    recv = [recv_early, recv_soon, recv_late]
    scores = late_part(own_late, comps)
    parts, row_means, means_part = last_part(at, scalar(col), own, recv, (*early, *soon, scores, permute(scores, swap)))
    parts = lax.all_to_all(parts, "bcol", 0, 0, tiled=True)
    covariance = gram(at, own, recv, row_means)
    projected = jnp.sum(parts, axis=0).T
    return covariance, projected, means_part[0]


def solution(mesh):
    return jax.shard_map(
        on_device,
        mesh=mesh,
        in_specs=(P(("brow", "bcol"), None), P("bcol", None)),
        out_specs=(P("brow", "bcol"), P(("brow", "bcol"), None), P(("brow", "bcol"))),
        check_vma=False,
    )
```

```python
import functools

import jax
import jax.numpy as jnp
from jax import lax
from jax.experimental import pallas as pl
from jax.experimental.pallas import tpu as pltpu
from jax.sharding import PartitionSpec as P

F32 = jnp.float32
BF16 = jnp.bfloat16
AXES = ("brow", "bcol")
SCANS = 2048
PIXELS = 16384
COMPS = 256
LOCAL = 16
PANEL = 2048
HALF = 1024
STEPS = (0, 1, -1, 2)
ANY = pl.BlockSpec(memory_space=pl.ANY)
IN_VMEM = pl.BlockSpec(memory_space=pltpu.VMEM)
IN_SMEM = pl.BlockSpec(memory_space=pltpu.SMEM)
MIDDLE = pltpu.CompilerParams(vmem_limit_bytes=20 << 20)
SMALL = pltpu.CompilerParams(vmem_limit_bytes=8 << 20)


def flat(x, y, z, k):
    return (((x // 2) * 4 + y) * 2 + k) * 8 + (x % 2) * 4 + z


def permute(value, move):
    pairs = []
    for x in range(4):
        for y in range(4):
            for z in range(4):
                for k in range(2):
                    x2, y2, z2, k2 = move(x, y, z, k)
                    pairs.append((flat(x, y, z, k), flat(x2, y2 % 4, z2 % 4, k2)))
    return lax.ppermute(value, AXES, pairs)


def spread(d):
    return lambda x, y, z, k: (x, y + d, z, k) if k == 0 else (x, y, z + d, k)


def across(m):
    return lambda x, y, z, k: (x ^ m, y, z, k)


def around(d):
    return lambda x, y, z, k: (x, y, z + d, k) if k == 0 else (x, y + d, z, k)


def swap(x, y, z, k):
    return x, y, z, 1 - k


def span_of(place, n, half):
    start = (half * 4 + lax.rem(place[0] + STEPS[n] + 4, 4)) * PANEL
    return pl.ds(pl.multiple_of(start, PANEL), PANEL)


def pick_kernel(place, mine, *refs):
    pieces, sems = refs[:4], refs[4]
    copies = []
    for n, piece in enumerate(pieces):
        for half in range(2):
            span = span_of(place, n, half)
            copies.append(pltpu.make_async_copy(mine.at[:, span], piece.at[half], sems.at[2 * n + half]))
            copies[-1].start()
    for copy in copies:
        copy.wait()


def pick(at, mine):
    return pl.pallas_call(
        pick_kernel,
        out_shape=[jax.ShapeDtypeStruct((2, LOCAL, PANEL), BF16)] * 4,
        in_specs=[IN_SMEM, ANY],
        out_specs=[IN_VMEM] * 4,
        scratch_shapes=[pltpu.SemaphoreType.DMA((8,))],
        compiler_params=SMALL,
    )(at, mine)


def join_kernel(place, other, *refs):
    for n, (mine, piece) in enumerate(zip(refs[:4], refs[4:])):
        for half in range(2):
            span = span_of(place, n, half)
            piece[half, 0] = mine[half]
            piece[half, 1] = other[:, span]


def join(at, other, mine):
    return pl.pallas_call(
        join_kernel,
        out_shape=[jax.ShapeDtypeStruct((2, 2, LOCAL, PANEL), BF16)] * 4,
        in_specs=[IN_SMEM] + [IN_VMEM] * 5,
        out_specs=[IN_VMEM] * 4,
        compiler_params=SMALL,
    )(at, other, *mine)


def group_kernel(core, own_half, *refs):
    pieces, groups = refs[:4], refs[4:]
    half = own_half[0]
    crossed = half + core[0] - 2 * half * core[0]
    for group, choice in zip(groups, (half, crossed, 1 - crossed, 1 - half)):
        for i, piece in enumerate(pieces):
            for source in range(2):
                group[source, i] = piece[choice, source]


def group(core, own_half, pieces):
    return pl.pallas_call(
        group_kernel,
        out_shape=[jax.ShapeDtypeStruct((2, 4, LOCAL, PANEL), BF16)] * 4,
        in_specs=[IN_SMEM] * 2 + [IN_VMEM] * 4,
        out_specs=[IN_VMEM] * 4,
        compiler_params=SMALL,
    )(core, own_half, *pieces)


def pack_kernel(plan, *refs):
    sources, packed = refs[: -len(plan)], refs[-len(plan) :]
    for out, parts in zip(packed, plan):
        at = 0
        for n, first, last in parts:
            out[at : at + last - first] = sources[n][first:last]
            at += last - first


def pack(plan, *sources):
    sizes = [sum(last - first for _, first, last in parts) for parts in plan]
    return pl.pallas_call(
        functools.partial(pack_kernel, plan),
        out_shape=[jax.ShapeDtypeStruct((size, 4, LOCAL, PANEL), BF16) for size in sizes],
        in_specs=[IN_VMEM] * len(sources),
        out_specs=[IN_VMEM] * len(sizes),
        compiler_params=SMALL,
    )(*sources)


EARLY = [(0, 0), (0, 1), (0, 2), (1, 0), (2, 0)]
SOON = [(0, 3), (1, 1), (2, 1), (1, 2), (2, 2), (3, 0)]
LATE = [(1, 3), (3, 1), (2, 3), (3, 2), (3, 3)]
ORDER = (EARLY, SOON, LATE)
WIDTH = 128
LEFT = (((0,), (0,)), ((), ()))


def fetch(core, own, recv, rows, cols, sems):
    def start(row_from, col_from, offset):
        for row, col, labels in zip(row_from, col_from, ORDER):
            for i, (m, step) in enumerate(labels):
                pltpu.make_async_copy(col.at[i], cols.at[m, step], sems.at[m]).start()
                for s in range(2):
                    pltpu.make_async_copy(
                        row.at[i, s, :, :, pl.ds(offset, HALF)], rows.at[m, :, 1 - s, step], sems.at[m]
                    ).start()

    @pl.when(core == 0)
    def _():
        start(own, recv, 0)

    @pl.when(core == 1)
    def _():
        start(recv, own, HALF)


def fetched(own, rows, cols, sems, which):
    for array, labels in zip(own, ORDER):
        for i, (m, step) in enumerate(labels):
            if m == which:
                pltpu.make_async_copy(array.at[i], cols.at[m, step], sems.at[m]).wait()
                for s in range(2):
                    pltpu.make_async_copy(
                        array.at[i, s, :, :, pl.ds(0, HALF)], rows.at[m, :, 1 - s, step], sems.at[m]
                    ).wait()


ROWS = pltpu.VMEM((4, 4, 2, 4, LOCAL, HALF), BF16)
COLS = pltpu.VMEM((4, 4, 2, 4, LOCAL, PANEL), BF16)


def ones_beside(block):
    return jnp.concatenate([block, jnp.ones((block.shape[0], 128), BF16)], axis=1)


def score_of(comps, block):
    score = jnp.dot(block, comps, preferred_element_type=F32)
    return (score[:, :COMPS] + score[:, COMPS:]).T


def left_of(centred):
    high = centred.astype(BF16)
    low = (centred - high.astype(F32)).astype(BF16)
    return jnp.concatenate([high, low, jnp.ones((16, centred.shape[1]), BF16)], axis=0)


def product_of(left, panel):
    product = jnp.dot(left, panel, preferred_element_type=F32)
    return product[:COMPS] + product[COMPS : 2 * COMPS], product[2 * COMPS : 2 * COMPS + 1]


def select(core, own, recv, use):
    @pl.when(core == 0)
    def _():
        use(own, recv, 0)

    @pl.when(core == 1)
    def _():
        use(recv, own, HALF)


def early_kernel(at, own, recv, components, scores, origin, comps, cols):
    comps[:, :COMPS] = components[...].astype(BF16)
    comps[:, COMPS:] = (components[...] - comps[:, :COMPS].astype(F32)).astype(BF16)

    def use(row_from, col_from, offset):
        cols[...] = col_from[...]

    select(at[0], own, recv, use)
    score = score_of(comps[...], cols[...].reshape(len(EARLY) * WIDTH, PANEL))
    scores[...] = score
    mean = jnp.sum(score, axis=1, keepdims=True) * (1.0 / score.shape[1])
    origin[...] = jnp.broadcast_to(mean, (COMPS, 128))


def early_part(at, own, recv, comps):
    return pl.pallas_call(
        early_kernel,
        out_shape=[
            jax.ShapeDtypeStruct((COMPS, len(EARLY) * WIDTH), F32),
            jax.ShapeDtypeStruct((COMPS, 128), F32),
            jax.ShapeDtypeStruct((PANEL, 2 * COMPS), BF16),
        ],
        in_specs=[IN_SMEM] + [IN_VMEM] * 3,
        out_specs=[IN_VMEM] * 3,
        scratch_shapes=[pltpu.VMEM((len(EARLY), 2, 4, LOCAL, PANEL), BF16)],
        compiler_params=MIDDLE,
        cost_estimate=pl.CostEstimate(flops=1 << 30, bytes_accessed=1 << 20, transcendentals=0),
    )(at, own, recv, comps)


def find(arrays, m, step):
    for array, labels in zip(arrays, ORDER):
        if (m, step) in labels:
            return array, labels.index((m, step))


def soon_kernel(at, *refs):
    own, recv, comps, early, origin = refs[:2], refs[2:4], *refs[4:7]
    scores, total, row_sum, left_last, rows, cols = refs[7:]

    def use(row_from, col_from, offset):
        cols[...] = col_from[1][...]
        for m in range(3):
            for step in range(4 if m == 0 else 3):
                array, i = find(row_from, m, step)
                for s in range(2):
                    rows[m, :, 1 - s, step] = array[i, s, :, :, offset : offset + HALF]

    select(at[0], own, recv, use)
    rows[1:, :, :, 3] = jnp.zeros((2, 4, 2, LOCAL, HALF), BF16)
    score = score_of(comps[...], cols[...].reshape(len(SOON) * WIDTH, PANEL))
    scores[...] = score
    known = (early[...], score)

    def piece(m, step):
        block, i = find(known, m, step)
        return block[:, i * WIDTH : (i + 1) * WIDTH] - origin[:, :1]

    sums = []
    for m in range(3):
        steps = range(4 if m == 0 else 3)
        left = left_of(jnp.concatenate([piece(m, step) for step in steps], axis=1))
        sums.append(product_of(left, rows[m, : len(steps)].reshape(len(steps) * WIDTH, HALF)))
    total[...] = sums[0][0] + sums[1][0] + sums[2][0]
    row_sum[...] = sums[0][1] + sums[1][1] + sums[2][1]
    turned = (early[...].T, score.T)
    blocks = []
    for m in (1, 2):
        for step in range(3):
            block, i = find(turned, m, step)
            for s in range(2):
                start = i * WIDTH + (s * 4 + 3) * LOCAL
                blocks.append(block[start : start + LOCAL])
    blocks.append(jnp.zeros((4 * LOCAL, COMPS), F32))
    left_last[...] = left_of(jnp.concatenate(blocks, axis=0).T - origin[:, :1])


def soon_part(at, own, recv, comps, early):
    return pl.pallas_call(
        soon_kernel,
        out_shape=[
            jax.ShapeDtypeStruct((COMPS, len(SOON) * WIDTH), F32),
            jax.ShapeDtypeStruct((COMPS, HALF), F32),
            jax.ShapeDtypeStruct((1, HALF), F32),
            jax.ShapeDtypeStruct((2 * COMPS + 16, 2 * WIDTH), BF16),
        ],
        in_specs=[IN_SMEM] + [IN_VMEM] * 7,
        out_specs=[IN_VMEM] * 4,
        scratch_shapes=[
            pltpu.VMEM((3, 4, 2, 4, LOCAL, HALF), BF16),
            pltpu.VMEM((len(SOON), 2, 4, LOCAL, PANEL), BF16),
        ],
        compiler_params=MIDDLE,
        cost_estimate=pl.CostEstimate(flops=2 << 30, bytes_accessed=1 << 20, transcendentals=0),
    )(at, *own, *recv, comps, *early)


def late_kernel(own, comps, scores):
    scores[...] = score_of(comps[...], own[...].reshape(len(LATE) * WIDTH, PANEL))


def late_part(own, comps):
    return pl.pallas_call(
        late_kernel,
        out_shape=jax.ShapeDtypeStruct((COMPS, len(LATE) * WIDTH), F32),
        in_specs=[IN_VMEM] * 2,
        out_specs=IN_VMEM,
        compiler_params=SMALL,
        cost_estimate=pl.CostEstimate(flops=1 << 30, bytes_accessed=1 << 20, transcendentals=0),
    )(own, comps)


def last_kernel(at, column, *refs):
    own, recv, early, origin, soon, total_in, rs_in, left_in = refs[:3], refs[3:6], *refs[6:12]
    late_own, late_recv, parts, means, means_part, rows, left = refs[12:]

    def put(place, scores, m, step):
        block, i = find(scores, m, step)
        left[:, place : place + WIDTH] = left_of(block[:, i * WIDTH : (i + 1) * WIDTH] - origin[:, :1])

    def use(row_from, col_from, offset):
        def row(m, step, s, spread):
            array, i = find(row_from, m, step)
            return array[i, 1 - s, spread, :, offset : offset + HALF]

        for s in range(2):
            for m in (1, 2):
                for c in range(3):
                    rows[((m - 1) * 3 + c) * 2 + s] = row(m, 3, s, c)
                for step in range(4):
                    rows[8 + m * 8 + s * 4 + step] = row(m, step, s, 3)
            for c in range(4):
                for step in range(4):
                    rows[32 + c * 8 + s * 4 + step] = row(3, step, s, c)
        scores = (early, soon, late_recv if offset == 0 else late_own)
        for m in (1, 2):
            put((m + 1) * WIDTH, scores, m, 3)
        for c in range(4):
            put((4 + c) * WIDTH, scores, 3, c)

    select(at[0], own, recv, use)
    rows[12:16] = jnp.zeros((4, LOCAL, HALF), BF16)
    left[:, : 2 * WIDTH] = left_in[...]
    late = jnp.where(at[0] == 0, late_recv[...], late_own[...])
    score_sum = sum(jnp.sum(block, axis=1, keepdims=True) for block in (early[...], soon[...], late))
    total, row_sum = product_of(left[...], rows[...].reshape(8 * WIDTH, HALF))
    row_sum = row_sum + rs_in[...]
    shift = score_sum * (1.0 / SCANS) - origin[:, :1]
    total = (total + total_in[...] - shift * row_sum) * (1.0 / (SCANS - 1))
    for c in range(8):
        parts[c] = total[:, c * 128 : (c + 1) * 128]
    means[...] = row_sum * (1.0 / SCANS)
    means_part[...] = means[:, pl.ds(pl.multiple_of(column[0] * 128, 128), 128)]


def last_part(at, column, own, recv, state):
    return pl.pallas_call(
        last_kernel,
        out_shape=[
            jax.ShapeDtypeStruct((8, COMPS, 128), F32),
            jax.ShapeDtypeStruct((1, HALF), F32),
            jax.ShapeDtypeStruct((1, 128), F32),
        ],
        in_specs=[IN_SMEM] * 2 + [IN_VMEM] * 14,
        out_specs=[IN_VMEM] * 3,
        scratch_shapes=[
            pltpu.VMEM((64, LOCAL, HALF), BF16),
            pltpu.VMEM((2 * COMPS + 16, 8 * WIDTH), BF16),
        ],
        compiler_params=MIDDLE,
        cost_estimate=pl.CostEstimate(flops=4 << 30, bytes_accessed=4 << 20, transcendentals=0),
    )(at, column, *own, *recv, *state)


def gram_kernel(at, *refs):
    own, recv, row_means, out = refs[:3], refs[3:6], refs[6], refs[7]
    rows, cols, stage, col_sums, sems, out_sems = refs[8:]
    fetch(at[0], own, recv, rows, cols, sems)
    copies = []
    for i in range(4):
        slot = i % 2
        if i >= 2:
            copies[i - 2].wait()
        span_i = slice(i * 256, (i + 1) * 256)
        row_mean = jnp.transpose(jnp.broadcast_to(row_means[:, span_i], (128, 256)))[:, :1]
        if i == 0:
            for m in range(4):
                fetched(own, rows, cols, sems, m)
                left = ones_beside(rows[m, :, :, :, :, span_i].reshape(512, 256))
                for j in range(8):
                    span = slice(j * 256, (j + 1) * 256)
                    right = cols[m, :, :, :, :, span].reshape(512, 256)
                    both = lax.dot_general(left, right, LEFT, preferred_element_type=F32)
                    tile, col_sum = both[:256], both[256:257]
                    if m > 0:
                        tile += stage[slot, :, span]
                        col_sum += col_sums[:, span]
                    if m == 3:
                        tile = (tile - row_mean * col_sum) * (1.0 / (SCANS - 1))
                    stage[slot, :, span] = tile
                    col_sums[:, span] = col_sum
        else:
            left = rows[:, :, :, :, :, span_i].reshape(SCANS, 256)
            for j in range(8):
                span = slice(j * 256, (j + 1) * 256)
                right = cols[:, :, :, :, :, span].reshape(SCANS, 256)
                tile = lax.dot_general(left, right, LEFT, preferred_element_type=F32)
                stage[slot, :, span] = (tile - row_mean * col_sums[:, span]) * (1.0 / (SCANS - 1))
        copy = pltpu.make_async_copy(stage.at[slot], out.at[pl.ds(i * 256, 256), :], out_sems.at[slot])
        copy.start()
        copies.append(copy)
    for copy in copies[2:]:
        copy.wait()


def gram(at, own, recv, row_means):
    return pl.pallas_call(
        gram_kernel,
        out_shape=jax.ShapeDtypeStruct((HALF, PANEL), F32),
        in_specs=[IN_SMEM] + [ANY] * 6 + [IN_VMEM],
        out_specs=ANY,
        scratch_shapes=[
            ROWS,
            COLS,
            pltpu.VMEM((2, 256, PANEL), F32),
            pltpu.VMEM((1, PANEL), F32),
            pltpu.SemaphoreType.DMA((4,)),
            pltpu.SemaphoreType.DMA((2,)),
        ],
        compiler_params=pltpu.CompilerParams(vmem_limit_bytes=22 << 20),
        cost_estimate=pl.CostEstimate(flops=8 << 30, bytes_accessed=20 << 20, transcendentals=0),
    )(at, *[pltpu.with_memory_space_constraint(piece, pltpu.HBM) for piece in own + recv], row_means)


def scalar(value):
    return jnp.reshape(value, (1,)).astype(jnp.int32)


def on_device(patterns, components):
    row = lax.axis_index("brow")
    col = lax.axis_index("bcol")
    k, y, xh = row % 2, (row // 2) % 4, row // 8
    z, xl = col % 4, col // 4
    first = k == 0
    same = jnp.where(first, y, z)
    at = scalar(same)
    mine = pick(at, pltpu.with_memory_space_constraint(patterns, pltpu.HBM))
    sends = join(at, permute(patterns, swap), mine)
    got = {n: permute(sends[n], spread(STEPS[n])) for n in (3, 1, 2)}
    got = [sends[0]] + [got[n] for n in range(1, 4)]
    own_half = jnp.where(first, xh, xl)
    group_own, to_1, to_2, to_3 = group(scalar(k), scalar(own_half), got)
    at = scalar(k)
    near = [permute(to_1, across(1)), permute(to_3, across(3))]
    ring_own = [permute(group_own, around(d)) for d in STEPS[1:3]]
    near, ring_own, to_2 = lax.optimization_barrier((near, ring_own, to_2))
    far = permute(to_2, across(2))
    ring = pack((((0, 0, 2), (1, 0, 2), (2, 0, 1)), ((0, 0, 2), (1, 0, 2), (3, 1, 2))), *near, *ring_own)
    ring = [permute(ring[n], around(STEPS[n + 1])) for n in range(2)]
    (own_early,) = pack((tuple((n, 0, 2) for n in range(5)),), group_own, *ring_own, *near)
    own_early = own_early.reshape((5, 2, 4, LOCAL, PANEL))
    recv_early = permute(own_early, swap)
    *early, comps = early_part(at, own_early, recv_early, components)
    far, ring, early = lax.optimization_barrier((far, ring, early))
    late = pack((((0, 0, 2), (2, 0, 2)), ((1, 2, 4), (2, 0, 2))), *ring, far)
    opposite = permute(far, around(STEPS[3]))
    late = [permute(late[n], around(STEPS[n + 1])) for n in range(2)] + [opposite]
    (own_soon,) = pack((((0, 4, 5), (1, 4, 5), (0, 0, 4), (1, 0, 4), (2, 0, 2)),), *ring, far)
    own_soon = own_soon.reshape((6, 2, 4, LOCAL, PANEL))
    recv_soon = permute(own_soon, swap)
    soon = soon_part(at, (own_early, own_soon), (recv_early, recv_soon), comps, early)
    late, soon = lax.optimization_barrier((late, soon))
    (own_late,) = pack((((0, 0, 4), (1, 0, 4), (2, 0, 2)),), *late)
    own_late = own_late.reshape((5, 2, 4, LOCAL, PANEL))
    recv_late = permute(own_late, swap)
    own = [own_early, own_soon, own_late]
    recv = [recv_early, recv_soon, recv_late]
    scores = late_part(own_late, comps)
    parts, row_means, means_part = last_part(at, scalar(col), own, recv, (*early, *soon, scores, permute(scores, swap)))
    parts = lax.all_to_all(parts, "bcol", 0, 0, tiled=True)
    covariance = gram(at, own, recv, row_means)
    projected = jnp.sum(parts, axis=0).T
    return covariance, projected, means_part[0]


def solution(mesh):
    return jax.shard_map(
        on_device,
        mesh=mesh,
        in_specs=(P(("brow", "bcol"), None), P("bcol", None)),
        out_specs=(P("brow", "bcol"), P(("brow", "bcol"), None), P(("brow", "bcol"))),
        check_vma=False,
    )
```

```python
import functools

import jax
import jax.numpy as jnp
from jax import lax
from jax.experimental import pallas as pl
from jax.experimental.pallas import tpu as pltpu
from jax.sharding import PartitionSpec as P

F32 = jnp.float32
BF16 = jnp.bfloat16
AXES = ("brow", "bcol")
SCANS = 2048
PIXELS = 16384
COMPS = 256
LOCAL = 16
PANEL = 2048
HALF = 1024
STEPS = (0, 1, -1, 2)
ANY = pl.BlockSpec(memory_space=pl.ANY)
IN_VMEM = pl.BlockSpec(memory_space=pltpu.VMEM)
IN_SMEM = pl.BlockSpec(memory_space=pltpu.SMEM)
MIDDLE = pltpu.CompilerParams(vmem_limit_bytes=20 << 20)
SMALL = pltpu.CompilerParams(vmem_limit_bytes=8 << 20)


def flat(x, y, z, k):
    return (((x // 2) * 4 + y) * 2 + k) * 8 + (x % 2) * 4 + z


def permute(value, move):
    pairs = []
    for x in range(4):
        for y in range(4):
            for z in range(4):
                for k in range(2):
                    x2, y2, z2, k2 = move(x, y, z, k)
                    pairs.append((flat(x, y, z, k), flat(x2, y2 % 4, z2 % 4, k2)))
    return lax.ppermute(value, AXES, pairs)


def spread(d):
    return lambda x, y, z, k: (x, y + d, z, k) if k == 0 else (x, y, z + d, k)


def across(m):
    return lambda x, y, z, k: (x ^ m, y, z, k)


def around(d):
    return lambda x, y, z, k: (x, y, z + d, k) if k == 0 else (x, y + d, z, k)


def swap(x, y, z, k):
    return x, y, z, 1 - k


def span_of(place, n, half):
    start = (half * 4 + lax.rem(place[0] + STEPS[n] + 4, 4)) * PANEL
    return pl.ds(pl.multiple_of(start, PANEL), PANEL)


def pick_kernel(place, mine, *refs):
    pieces, sems = refs[:4], refs[4]
    copies = []
    for n, piece in enumerate(pieces):
        for half in range(2):
            span = span_of(place, n, half)
            copies.append(pltpu.make_async_copy(mine.at[:, span], piece.at[half], sems.at[2 * n + half]))
            copies[-1].start()
    for copy in copies:
        copy.wait()


def pick(at, mine):
    return pl.pallas_call(
        pick_kernel,
        out_shape=[jax.ShapeDtypeStruct((2, LOCAL, PANEL), BF16)] * 4,
        in_specs=[IN_SMEM, ANY],
        out_specs=[IN_VMEM] * 4,
        scratch_shapes=[pltpu.SemaphoreType.DMA((8,))],
        compiler_params=SMALL,
    )(at, mine)


def join_kernel(place, other, *refs):
    for n, (mine, piece) in enumerate(zip(refs[:4], refs[4:])):
        for half in range(2):
            span = span_of(place, n, half)
            piece[half, 0] = mine[half]
            piece[half, 1] = other[:, span]


def join(at, other, mine):
    return pl.pallas_call(
        join_kernel,
        out_shape=[jax.ShapeDtypeStruct((2, 2, LOCAL, PANEL), BF16)] * 4,
        in_specs=[IN_SMEM] + [IN_VMEM] * 5,
        out_specs=[IN_VMEM] * 4,
        compiler_params=SMALL,
    )(at, other, *mine)


def group_kernel(core, own_half, *refs):
    pieces, groups = refs[:4], refs[4:]
    half = own_half[0]
    crossed = half + core[0] - 2 * half * core[0]
    for group, choice in zip(groups, (half, crossed, 1 - crossed, 1 - half)):
        for i, piece in enumerate(pieces):
            for source in range(2):
                group[source, i] = piece[choice, source]


def group(core, own_half, pieces):
    return pl.pallas_call(
        group_kernel,
        out_shape=[jax.ShapeDtypeStruct((2, 4, LOCAL, PANEL), BF16)] * 4,
        in_specs=[IN_SMEM] * 2 + [IN_VMEM] * 4,
        out_specs=[IN_VMEM] * 4,
        compiler_params=SMALL,
    )(core, own_half, *pieces)


def pack_kernel(plan, *refs):
    sources, packed = refs[: -len(plan)], refs[-len(plan) :]
    for out, parts in zip(packed, plan):
        at = 0
        for n, first, last in parts:
            out[at : at + last - first] = sources[n][first:last]
            at += last - first


def pack(plan, *sources):
    sizes = [sum(last - first for _, first, last in parts) for parts in plan]
    return pl.pallas_call(
        functools.partial(pack_kernel, plan),
        out_shape=[jax.ShapeDtypeStruct((size, 4, LOCAL, PANEL), BF16) for size in sizes],
        in_specs=[IN_VMEM] * len(sources),
        out_specs=[IN_VMEM] * len(sizes),
        compiler_params=SMALL,
    )(*sources)


EARLY = [(0, 0), (0, 1), (0, 2), (1, 0), (2, 0)]
SOON = [(0, 3), (1, 1), (2, 1), (1, 2), (2, 2), (3, 0)]
LATE = [(1, 3), (3, 1), (2, 3), (3, 2), (3, 3)]
ORDER = (EARLY, SOON, LATE)
WIDTH = 128
LEFT = (((0,), (0,)), ((), ()))


def fetch(core, own, recv, rows, cols, sems):
    def start(row_from, col_from, offset):
        for row, col, labels in zip(row_from, col_from, ORDER):
            for i, (m, step) in enumerate(labels):
                pltpu.make_async_copy(col.at[i], cols.at[m, step], sems.at[m]).start()
                for s in range(2):
                    pltpu.make_async_copy(
                        row.at[i, s, :, :, pl.ds(offset, HALF)], rows.at[m, :, 1 - s, step], sems.at[m]
                    ).start()

    @pl.when(core == 0)
    def _():
        start(own, recv, 0)

    @pl.when(core == 1)
    def _():
        start(recv, own, HALF)


def fetched(own, rows, cols, sems, which):
    for array, labels in zip(own, ORDER):
        for i, (m, step) in enumerate(labels):
            if m == which:
                pltpu.make_async_copy(array.at[i], cols.at[m, step], sems.at[m]).wait()
                for s in range(2):
                    pltpu.make_async_copy(
                        array.at[i, s, :, :, pl.ds(0, HALF)], rows.at[m, :, 1 - s, step], sems.at[m]
                    ).wait()


ROWS = pltpu.VMEM((4, 4, 2, 4, LOCAL, HALF), BF16)
COLS = pltpu.VMEM((4, 4, 2, 4, LOCAL, PANEL), BF16)


def ones_beside(block):
    return jnp.concatenate([block, jnp.ones((block.shape[0], 16), BF16)], axis=1)


def score_of(comps, block):
    score = jnp.dot(block, comps, preferred_element_type=F32)
    return (score[:, :COMPS] + score[:, COMPS:]).T


def left_of(centred):
    high = centred.astype(BF16)
    low = (centred - high.astype(F32)).astype(BF16)
    return jnp.concatenate([high, low, jnp.ones((16, centred.shape[1]), BF16)], axis=0)


def product_of(left, panel):
    product = jnp.dot(left, panel, preferred_element_type=F32)
    return product[:COMPS] + product[COMPS : 2 * COMPS], product[2 * COMPS : 2 * COMPS + 1]


def select(core, own, recv, use):
    @pl.when(core == 0)
    def _():
        use(own, recv, 0)

    @pl.when(core == 1)
    def _():
        use(recv, own, HALF)


def early_kernel(at, own, recv, components, scores, origin, comps, cols):
    comps[:, :COMPS] = components[...].astype(BF16)
    comps[:, COMPS:] = (components[...] - comps[:, :COMPS].astype(F32)).astype(BF16)

    def use(row_from, col_from, offset):
        cols[...] = col_from[...]

    select(at[0], own, recv, use)
    score = score_of(comps[...], cols[...].reshape(len(EARLY) * WIDTH, PANEL))
    scores[...] = score
    mean = jnp.sum(score, axis=1, keepdims=True) * (1.0 / score.shape[1])
    origin[...] = jnp.broadcast_to(mean, (COMPS, 128))


def early_part(at, own, recv, comps):
    return pl.pallas_call(
        early_kernel,
        out_shape=[
            jax.ShapeDtypeStruct((COMPS, len(EARLY) * WIDTH), F32),
            jax.ShapeDtypeStruct((COMPS, 128), F32),
            jax.ShapeDtypeStruct((PANEL, 2 * COMPS), BF16),
        ],
        in_specs=[IN_SMEM] + [IN_VMEM] * 3,
        out_specs=[IN_VMEM] * 3,
        scratch_shapes=[pltpu.VMEM((len(EARLY), 2, 4, LOCAL, PANEL), BF16)],
        compiler_params=MIDDLE,
        cost_estimate=pl.CostEstimate(flops=1 << 30, bytes_accessed=1 << 20, transcendentals=0),
    )(at, own, recv, comps)


def find(arrays, m, step):
    for array, labels in zip(arrays, ORDER):
        if (m, step) in labels:
            return array, labels.index((m, step))


def soon_kernel(at, *refs):
    own, recv, comps, early, origin = refs[:2], refs[2:4], *refs[4:7]
    scores, total, row_sum, left_last, rows, cols = refs[7:]

    def use(row_from, col_from, offset):
        cols[...] = col_from[1][...]
        for m in range(3):
            for step in range(4 if m == 0 else 3):
                array, i = find(row_from, m, step)
                for s in range(2):
                    rows[m, :, 1 - s, step] = array[i, s, :, :, offset : offset + HALF]

    select(at[0], own, recv, use)
    rows[1:, :, :, 3] = jnp.zeros((2, 4, 2, LOCAL, HALF), BF16)
    score = score_of(comps[...], cols[...].reshape(len(SOON) * WIDTH, PANEL))
    scores[...] = score
    known = (early[...], score)

    def piece(m, step):
        block, i = find(known, m, step)
        return block[:, i * WIDTH : (i + 1) * WIDTH] - origin[:, :1]

    sums = []
    for m in range(3):
        steps = range(4 if m == 0 else 3)
        left = left_of(jnp.concatenate([piece(m, step) for step in steps], axis=1))
        sums.append(product_of(left, rows[m, : len(steps)].reshape(len(steps) * WIDTH, HALF)))
    total[...] = sums[0][0] + sums[1][0] + sums[2][0]
    row_sum[...] = sums[0][1] + sums[1][1] + sums[2][1]
    turned = (early[...].T, score.T)
    blocks = []
    for m in (1, 2):
        for step in range(3):
            block, i = find(turned, m, step)
            for s in range(2):
                start = i * WIDTH + (s * 4 + 3) * LOCAL
                blocks.append(block[start : start + LOCAL])
    blocks.append(jnp.zeros((4 * LOCAL, COMPS), F32))
    left_last[...] = left_of(jnp.concatenate(blocks, axis=0).T - origin[:, :1])


def soon_part(at, own, recv, comps, early):
    return pl.pallas_call(
        soon_kernel,
        out_shape=[
            jax.ShapeDtypeStruct((COMPS, len(SOON) * WIDTH), F32),
            jax.ShapeDtypeStruct((COMPS, HALF), F32),
            jax.ShapeDtypeStruct((1, HALF), F32),
            jax.ShapeDtypeStruct((2 * COMPS + 16, 2 * WIDTH), BF16),
        ],
        in_specs=[IN_SMEM] + [IN_VMEM] * 7,
        out_specs=[IN_VMEM] * 4,
        scratch_shapes=[
            pltpu.VMEM((3, 4, 2, 4, LOCAL, HALF), BF16),
            pltpu.VMEM((len(SOON), 2, 4, LOCAL, PANEL), BF16),
        ],
        compiler_params=MIDDLE,
        cost_estimate=pl.CostEstimate(flops=2 << 30, bytes_accessed=1 << 20, transcendentals=0),
    )(at, *own, *recv, comps, *early)


def late_kernel(own, comps, scores):
    scores[...] = score_of(comps[...], own[...].reshape(len(LATE) * WIDTH, PANEL))


def late_part(own, comps):
    return pl.pallas_call(
        late_kernel,
        out_shape=jax.ShapeDtypeStruct((COMPS, len(LATE) * WIDTH), F32),
        in_specs=[IN_VMEM] * 2,
        out_specs=IN_VMEM,
        compiler_params=SMALL,
        cost_estimate=pl.CostEstimate(flops=1 << 30, bytes_accessed=1 << 20, transcendentals=0),
    )(own, comps)


def last_kernel(at, column, *refs):
    own, recv, early, origin, soon, total_in, rs_in, left_in = refs[:3], refs[3:6], *refs[6:12]
    late_own, late_recv, parts, means, means_part, rows, left = refs[12:]

    def put(place, scores, m, step):
        block, i = find(scores, m, step)
        left[:, place : place + WIDTH] = left_of(block[:, i * WIDTH : (i + 1) * WIDTH] - origin[:, :1])

    def use(row_from, col_from, offset):
        def row(m, step, s, spread):
            array, i = find(row_from, m, step)
            return array[i, 1 - s, spread, :, offset : offset + HALF]

        for s in range(2):
            for m in (1, 2):
                for c in range(3):
                    rows[((m - 1) * 3 + c) * 2 + s] = row(m, 3, s, c)
                for step in range(4):
                    rows[8 + m * 8 + s * 4 + step] = row(m, step, s, 3)
            for c in range(4):
                for step in range(4):
                    rows[32 + c * 8 + s * 4 + step] = row(3, step, s, c)
        scores = (early, soon, late_recv if offset == 0 else late_own)
        for m in (1, 2):
            put((m + 1) * WIDTH, scores, m, 3)
        for c in range(4):
            put((4 + c) * WIDTH, scores, 3, c)

    select(at[0], own, recv, use)
    rows[12:16] = jnp.zeros((4, LOCAL, HALF), BF16)
    left[:, : 2 * WIDTH] = left_in[...]
    late = jnp.where(at[0] == 0, late_recv[...], late_own[...])
    score_sum = sum(jnp.sum(block, axis=1, keepdims=True) for block in (early[...], soon[...], late))
    total, row_sum = product_of(left[...], rows[...].reshape(8 * WIDTH, HALF))
    row_sum = row_sum + rs_in[...]
    shift = score_sum * (1.0 / SCANS) - origin[:, :1]
    total = (total + total_in[...] - shift * row_sum) * (1.0 / (SCANS - 1))
    for c in range(8):
        parts[c] = total[:, c * 128 : (c + 1) * 128]
    means[...] = row_sum * (1.0 / SCANS)
    means_part[...] = means[:, pl.ds(pl.multiple_of(column[0] * 128, 128), 128)]


def last_part(at, column, own, recv, state):
    return pl.pallas_call(
        last_kernel,
        out_shape=[
            jax.ShapeDtypeStruct((8, COMPS, 128), F32),
            jax.ShapeDtypeStruct((1, HALF), F32),
            jax.ShapeDtypeStruct((1, 128), F32),
        ],
        in_specs=[IN_SMEM] * 2 + [IN_VMEM] * 14,
        out_specs=[IN_VMEM] * 3,
        scratch_shapes=[
            pltpu.VMEM((64, LOCAL, HALF), BF16),
            pltpu.VMEM((2 * COMPS + 16, 8 * WIDTH), BF16),
        ],
        compiler_params=MIDDLE,
        cost_estimate=pl.CostEstimate(flops=4 << 30, bytes_accessed=4 << 20, transcendentals=0),
    )(at, column, *own, *recv, *state)


def gram_kernel(at, *refs):
    own, recv, row_means, out = refs[:3], refs[3:6], refs[6], refs[7]
    rows, cols, stage, col_sums, sems, out_sems = refs[8:]
    fetch(at[0], own, recv, rows, cols, sems)
    copies = []
    for i in range(4):
        slot = i % 2
        if i >= 2:
            copies[i - 2].wait()
        span_i = slice(i * 256, (i + 1) * 256)
        row_mean = jnp.transpose(jnp.broadcast_to(row_means[:, span_i], (128, 256)))[:, :1]
        if i == 0:
            for m in range(4):
                fetched(own, rows, cols, sems, m)
                left = ones_beside(rows[m, :, :, :, :, span_i].reshape(512, 256))
                for j in range(8):
                    span = slice(j * 256, (j + 1) * 256)
                    right = cols[m, :, :, :, :, span].reshape(512, 256)
                    both = lax.dot_general(left, right, LEFT, preferred_element_type=F32)
                    tile, col_sum = both[:256], both[256:257]
                    if m > 0:
                        tile += stage[slot, :, span]
                        col_sum += col_sums[:, span]
                    if m == 3:
                        tile = (tile - row_mean * col_sum) * (1.0 / (SCANS - 1))
                    stage[slot, :, span] = tile
                    col_sums[:, span] = col_sum
        else:
            left = rows[:, :, :, :, :, span_i].reshape(SCANS, 256)
            for j in range(8):
                span = slice(j * 256, (j + 1) * 256)
                right = cols[:, :, :, :, :, span].reshape(SCANS, 256)
                tile = lax.dot_general(left, right, LEFT, preferred_element_type=F32)
                stage[slot, :, span] = (tile - row_mean * col_sums[:, span]) * (1.0 / (SCANS - 1))
        copy = pltpu.make_async_copy(stage.at[slot], out.at[pl.ds(i * 256, 256), :], out_sems.at[slot])
        copy.start()
        copies.append(copy)
    for copy in copies[2:]:
        copy.wait()


def gram(at, own, recv, row_means):
    return pl.pallas_call(
        gram_kernel,
        out_shape=jax.ShapeDtypeStruct((HALF, PANEL), F32),
        in_specs=[IN_SMEM] + [ANY] * 6 + [IN_VMEM],
        out_specs=ANY,
        scratch_shapes=[
            ROWS,
            COLS,
            pltpu.VMEM((2, 256, PANEL), F32),
            pltpu.VMEM((1, PANEL), F32),
            pltpu.SemaphoreType.DMA((4,)),
            pltpu.SemaphoreType.DMA((2,)),
        ],
        compiler_params=pltpu.CompilerParams(vmem_limit_bytes=22 << 20),
        cost_estimate=pl.CostEstimate(flops=8 << 30, bytes_accessed=20 << 20, transcendentals=0),
    )(at, *[pltpu.with_memory_space_constraint(piece, pltpu.HBM) for piece in own + recv], row_means)


def scalar(value):
    return jnp.reshape(value, (1,)).astype(jnp.int32)


def on_device(patterns, components):
    row = lax.axis_index("brow")
    col = lax.axis_index("bcol")
    k, y, xh = row % 2, (row // 2) % 4, row // 8
    z, xl = col % 4, col // 4
    first = k == 0
    same = jnp.where(first, y, z)
    at = scalar(same)
    mine = pick(at, pltpu.with_memory_space_constraint(patterns, pltpu.HBM))
    sends = join(at, permute(patterns, swap), mine)
    got = {n: permute(sends[n], spread(STEPS[n])) for n in (3, 1, 2)}
    got = [sends[0]] + [got[n] for n in range(1, 4)]
    own_half = jnp.where(first, xh, xl)
    group_own, to_1, to_2, to_3 = group(scalar(k), scalar(own_half), got)
    at = scalar(k)
    near = [permute(to_1, across(1)), permute(to_3, across(3))]
    ring_own = [permute(group_own, around(d)) for d in STEPS[1:3]]
    near, ring_own, to_2 = lax.optimization_barrier((near, ring_own, to_2))
    far = permute(to_2, across(2))
    ring = pack((((0, 0, 2), (1, 0, 2), (2, 0, 1)), ((0, 0, 2), (1, 0, 2), (3, 1, 2))), *near, *ring_own)
    ring = [permute(ring[n], around(STEPS[n + 1])) for n in range(2)]
    (own_early,) = pack((tuple((n, 0, 2) for n in range(5)),), group_own, *ring_own, *near)
    own_early = own_early.reshape((5, 2, 4, LOCAL, PANEL))
    recv_early = permute(own_early, swap)
    *early, comps = early_part(at, own_early, recv_early, components)
    far, ring, early = lax.optimization_barrier((far, ring, early))
    late = pack((((0, 0, 2), (2, 0, 2)), ((1, 2, 4), (2, 0, 2))), *ring, far)
    opposite = permute(far, around(STEPS[3]))
    late = [permute(late[n], around(STEPS[n + 1])) for n in range(2)] + [opposite]
    (own_soon,) = pack((((0, 4, 5), (1, 4, 5), (0, 0, 4), (1, 0, 4), (2, 0, 2)),), *ring, far)
    own_soon = own_soon.reshape((6, 2, 4, LOCAL, PANEL))
    recv_soon = permute(own_soon, swap)
    soon = soon_part(at, (own_early, own_soon), (recv_early, recv_soon), comps, early)
    late, soon = lax.optimization_barrier((late, soon))
    (own_late,) = pack((((0, 0, 4), (1, 0, 4), (2, 0, 2)),), *late)
    own_late = own_late.reshape((5, 2, 4, LOCAL, PANEL))
    recv_late = permute(own_late, swap)
    own = [own_early, own_soon, own_late]
    recv = [recv_early, recv_soon, recv_late]
    scores = late_part(own_late, comps)
    parts, row_means, means_part = last_part(at, scalar(col), own, recv, (*early, *soon, scores, permute(scores, swap)))
    parts = lax.all_to_all(parts, "bcol", 0, 0, tiled=True)
    covariance = gram(at, own, recv, row_means)
    projected = jnp.sum(parts, axis=0).T
    return covariance, projected, means_part[0]


def solution(mesh):
    return jax.shard_map(
        on_device,
        mesh=mesh,
        in_specs=(P(("brow", "bcol"), None), P("bcol", None)),
        out_specs=(P("brow", "bcol"), P(("brow", "bcol"), None), P(("brow", "bcol"))),
        check_vma=False,
    )
```

```python
import functools

import jax
import jax.numpy as jnp
from jax import lax
from jax.experimental import pallas as pl
from jax.experimental.pallas import tpu as pltpu
from jax.sharding import PartitionSpec as P

F32 = jnp.float32
BF16 = jnp.bfloat16
AXES = ("brow", "bcol")
SCANS = 2048
PIXELS = 16384
COMPS = 256
LOCAL = 16
PANEL = 2048
HALF = 1024
STEPS = (0, 1, -1, 2)
ANY = pl.BlockSpec(memory_space=pl.ANY)
IN_VMEM = pl.BlockSpec(memory_space=pltpu.VMEM)
IN_SMEM = pl.BlockSpec(memory_space=pltpu.SMEM)
MIDDLE = pltpu.CompilerParams(vmem_limit_bytes=20 << 20)
SMALL = pltpu.CompilerParams(vmem_limit_bytes=8 << 20)


def flat(x, y, z, k):
    return (((x // 2) * 4 + y) * 2 + k) * 8 + (x % 2) * 4 + z


def permute(value, move):
    pairs = []
    for x in range(4):
        for y in range(4):
            for z in range(4):
                for k in range(2):
                    x2, y2, z2, k2 = move(x, y, z, k)
                    pairs.append((flat(x, y, z, k), flat(x2, y2 % 4, z2 % 4, k2)))
    return lax.ppermute(value, AXES, pairs)


def spread(d):
    return lambda x, y, z, k: (x, y + d, z, k) if k == 0 else (x, y, z + d, k)


def across(m):
    return lambda x, y, z, k: (x ^ m, y, z, k)


def around(d):
    return lambda x, y, z, k: (x, y, z + d, k) if k == 0 else (x, y + d, z, k)


def swap(x, y, z, k):
    return x, y, z, 1 - k


def span_of(place, n, half):
    start = (half * 4 + lax.rem(place[0] + STEPS[n] + 4, 4)) * PANEL
    return pl.ds(pl.multiple_of(start, PANEL), PANEL)


def pick_kernel(place, mine, *refs):
    pieces, sems = refs[:4], refs[4]
    copies = []
    for n, piece in enumerate(pieces):
        for half in range(2):
            span = span_of(place, n, half)
            copies.append(pltpu.make_async_copy(mine.at[:, span], piece.at[half], sems.at[2 * n + half]))
            copies[-1].start()
    for copy in copies:
        copy.wait()


def pick(at, mine):
    return pl.pallas_call(
        pick_kernel,
        out_shape=[jax.ShapeDtypeStruct((2, LOCAL, PANEL), BF16)] * 4,
        in_specs=[IN_SMEM, ANY],
        out_specs=[IN_VMEM] * 4,
        scratch_shapes=[pltpu.SemaphoreType.DMA((8,))],
        compiler_params=SMALL,
    )(at, mine)


def join_kernel(place, other, *refs):
    for n, (mine, piece) in enumerate(zip(refs[:4], refs[4:])):
        for half in range(2):
            span = span_of(place, n, half)
            piece[half, 0] = mine[half]
            piece[half, 1] = other[:, span]


def join(at, other, mine):
    return pl.pallas_call(
        join_kernel,
        out_shape=[jax.ShapeDtypeStruct((2, 2, LOCAL, PANEL), BF16)] * 4,
        in_specs=[IN_SMEM] + [IN_VMEM] * 5,
        out_specs=[IN_VMEM] * 4,
        compiler_params=SMALL,
    )(at, other, *mine)


def group_kernel(core, own_half, *refs):
    pieces, groups = refs[:4], refs[4:]
    half = own_half[0]
    crossed = half + core[0] - 2 * half * core[0]
    for group, choice in zip(groups, (half, crossed, 1 - crossed, 1 - half)):
        for i, piece in enumerate(pieces):
            for source in range(2):
                group[source, i] = piece[choice, source]


def group(core, own_half, pieces):
    return pl.pallas_call(
        group_kernel,
        out_shape=[jax.ShapeDtypeStruct((2, 4, LOCAL, PANEL), BF16)] * 4,
        in_specs=[IN_SMEM] * 2 + [IN_VMEM] * 4,
        out_specs=[IN_VMEM] * 4,
        compiler_params=SMALL,
    )(core, own_half, *pieces)


def pack_kernel(plan, *refs):
    sources, packed = refs[: -len(plan)], refs[-len(plan) :]
    for out, parts in zip(packed, plan):
        at = 0
        for n, first, last in parts:
            out[at : at + last - first] = sources[n][first:last]
            at += last - first


def pack(plan, *sources):
    sizes = [sum(last - first for _, first, last in parts) for parts in plan]
    return pl.pallas_call(
        functools.partial(pack_kernel, plan),
        out_shape=[jax.ShapeDtypeStruct((size, 4, LOCAL, PANEL), BF16) for size in sizes],
        in_specs=[IN_VMEM] * len(sources),
        out_specs=[IN_VMEM] * len(sizes),
        compiler_params=SMALL,
    )(*sources)


EARLY = [(0, 0), (0, 1), (0, 2), (1, 0), (2, 0)]
SOON = [(0, 3), (1, 1), (2, 1), (1, 2), (2, 2), (3, 0)]
LATE = [(1, 3), (3, 1), (2, 3), (3, 2), (3, 3)]
ORDER = (EARLY, SOON, LATE)
WIDTH = 128
LEFT = (((0,), (0,)), ((), ()))


def fetch(core, own, recv, rows, cols, sems):
    def start(row_from, col_from, offset):
        for row, col, labels in zip(row_from, col_from, ORDER):
            for i, (m, step) in enumerate(labels):
                pltpu.make_async_copy(col.at[i], cols.at[m, step], sems.at[m]).start()
                for s in range(2):
                    pltpu.make_async_copy(
                        row.at[i, s, :, :, pl.ds(offset, HALF)], rows.at[m, :, 1 - s, step], sems.at[m]
                    ).start()

    @pl.when(core == 0)
    def _():
        start(own, recv, 0)

    @pl.when(core == 1)
    def _():
        start(recv, own, HALF)


def fetched(own, rows, cols, sems, which):
    for array, labels in zip(own, ORDER):
        for i, (m, step) in enumerate(labels):
            if m == which:
                pltpu.make_async_copy(array.at[i], cols.at[m, step], sems.at[m]).wait()
                for s in range(2):
                    pltpu.make_async_copy(
                        array.at[i, s, :, :, pl.ds(0, HALF)], rows.at[m, :, 1 - s, step], sems.at[m]
                    ).wait()


ROWS = pltpu.VMEM((4, 4, 2, 4, LOCAL, HALF), BF16)
COLS = pltpu.VMEM((4, 4, 2, 4, LOCAL, PANEL), BF16)


def ones_beside(block):
    return jnp.concatenate([block, jnp.ones((block.shape[0], 16), BF16)], axis=1)


def score_of(comps, block):
    score = jnp.dot(block, comps, preferred_element_type=F32)
    return (score[:, :COMPS] + score[:, COMPS:]).T


def left_of(centred):
    high = centred.astype(BF16)
    low = (centred - high.astype(F32)).astype(BF16)
    return jnp.concatenate([high, low, jnp.ones((16, centred.shape[1]), BF16)], axis=0)


def product_of(left, panel):
    product = jnp.dot(left, panel, preferred_element_type=F32)
    return product[:COMPS] + product[COMPS : 2 * COMPS], product[2 * COMPS : 2 * COMPS + 1]


def select(core, own, recv, use):
    @pl.when(core == 0)
    def _():
        use(own, recv, 0)

    @pl.when(core == 1)
    def _():
        use(recv, own, HALF)


def early_kernel(at, own, recv, components, scores, origin, comps, cols):
    comps[:, :COMPS] = components[...].astype(BF16)
    comps[:, COMPS:] = (components[...] - comps[:, :COMPS].astype(F32)).astype(BF16)

    def use(row_from, col_from, offset):
        cols[...] = col_from[...]

    select(at[0], own, recv, use)
    score = score_of(comps[...], cols[...].reshape(len(EARLY) * WIDTH, PANEL))
    scores[...] = score
    mean = jnp.sum(score, axis=1, keepdims=True) * (1.0 / score.shape[1])
    origin[...] = jnp.broadcast_to(mean, (COMPS, 128))


def early_part(at, own, recv, comps):
    return pl.pallas_call(
        early_kernel,
        out_shape=[
            jax.ShapeDtypeStruct((COMPS, len(EARLY) * WIDTH), F32),
            jax.ShapeDtypeStruct((COMPS, 128), F32),
            jax.ShapeDtypeStruct((PANEL, 2 * COMPS), BF16),
        ],
        in_specs=[IN_SMEM] + [IN_VMEM] * 3,
        out_specs=[IN_VMEM] * 3,
        scratch_shapes=[pltpu.VMEM((len(EARLY), 2, 4, LOCAL, PANEL), BF16)],
        compiler_params=MIDDLE,
        cost_estimate=pl.CostEstimate(flops=1 << 30, bytes_accessed=1 << 20, transcendentals=0),
    )(at, own, recv, comps)


def find(arrays, m, step):
    for array, labels in zip(arrays, ORDER):
        if (m, step) in labels:
            return array, labels.index((m, step))


def soon_kernel(at, *refs):
    own, recv, comps, early, origin = refs[:2], refs[2:4], *refs[4:7]
    scores, total, row_sum, left_last, rows, cols = refs[7:]

    def use(row_from, col_from, offset):
        cols[...] = col_from[1][...]
        for m in range(3):
            for step in range(4 if m == 0 else 3):
                array, i = find(row_from, m, step)
                for s in range(2):
                    rows[m, :, 1 - s, step] = array[i, s, :, :, offset : offset + HALF]

    select(at[0], own, recv, use)
    rows[1:, :, :, 3] = jnp.zeros((2, 4, 2, LOCAL, HALF), BF16)
    score = score_of(comps[...], cols[...].reshape(len(SOON) * WIDTH, PANEL))
    scores[...] = score
    known = (early[...], score)

    def piece(m, step):
        block, i = find(known, m, step)
        return block[:, i * WIDTH : (i + 1) * WIDTH] - origin[:, :1]

    sums = []
    for m in range(3):
        steps = range(4 if m == 0 else 3)
        left = left_of(jnp.concatenate([piece(m, step) for step in steps], axis=1))
        sums.append(product_of(left, rows[m, : len(steps)].reshape(len(steps) * WIDTH, HALF)))
    total[...] = sums[0][0] + sums[1][0] + sums[2][0]
    row_sum[...] = sums[0][1] + sums[1][1] + sums[2][1]
    turned = (early[...].T, score.T)
    blocks = []
    for m in (1, 2):
        for step in range(3):
            block, i = find(turned, m, step)
            for s in range(2):
                start = i * WIDTH + (s * 4 + 3) * LOCAL
                blocks.append(block[start : start + LOCAL])
    blocks.append(jnp.zeros((4 * LOCAL, COMPS), F32))
    left_last[...] = left_of(jnp.concatenate(blocks, axis=0).T - origin[:, :1])


def soon_part(at, own, recv, comps, early):
    return pl.pallas_call(
        soon_kernel,
        out_shape=[
            jax.ShapeDtypeStruct((COMPS, len(SOON) * WIDTH), F32),
            jax.ShapeDtypeStruct((COMPS, HALF), F32),
            jax.ShapeDtypeStruct((1, HALF), F32),
            jax.ShapeDtypeStruct((2 * COMPS + 16, 2 * WIDTH), BF16),
        ],
        in_specs=[IN_SMEM] + [IN_VMEM] * 7,
        out_specs=[IN_VMEM] * 4,
        scratch_shapes=[
            pltpu.VMEM((3, 4, 2, 4, LOCAL, HALF), BF16),
            pltpu.VMEM((len(SOON), 2, 4, LOCAL, PANEL), BF16),
        ],
        compiler_params=MIDDLE,
        cost_estimate=pl.CostEstimate(flops=2 << 30, bytes_accessed=1 << 20, transcendentals=0),
    )(at, *own, *recv, comps, *early)


def late_kernel(own, comps, scores):
    scores[...] = score_of(comps[...], own[...].reshape(len(LATE) * WIDTH, PANEL))


def late_part(own, comps):
    return pl.pallas_call(
        late_kernel,
        out_shape=jax.ShapeDtypeStruct((COMPS, len(LATE) * WIDTH), F32),
        in_specs=[IN_VMEM] * 2,
        out_specs=IN_VMEM,
        compiler_params=SMALL,
        cost_estimate=pl.CostEstimate(flops=1 << 30, bytes_accessed=1 << 20, transcendentals=0),
    )(own, comps)


def last_kernel(at, column, *refs):
    own, recv, early, origin, soon, total_in, rs_in, left_in = refs[:3], refs[3:6], *refs[6:12]
    late_own, late_recv, parts, means, means_part, rows, left = refs[12:]

    def put(place, scores, m, step):
        block, i = find(scores, m, step)
        left[:, place : place + WIDTH] = left_of(block[:, i * WIDTH : (i + 1) * WIDTH] - origin[:, :1])

    def use(row_from, col_from, offset):
        def row(m, step, s, spread):
            array, i = find(row_from, m, step)
            return array[i, 1 - s, spread, :, offset : offset + HALF]

        for s in range(2):
            for m in (1, 2):
                for c in range(3):
                    rows[((m - 1) * 3 + c) * 2 + s] = row(m, 3, s, c)
                for step in range(4):
                    rows[8 + m * 8 + s * 4 + step] = row(m, step, s, 3)
            for c in range(4):
                for step in range(4):
                    rows[32 + c * 8 + s * 4 + step] = row(3, step, s, c)
        scores = (early, soon, late_recv if offset == 0 else late_own)
        for m in (1, 2):
            put((m + 1) * WIDTH, scores, m, 3)
        for c in range(4):
            put((4 + c) * WIDTH, scores, 3, c)

    select(at[0], own, recv, use)
    rows[12:16] = jnp.zeros((4, LOCAL, HALF), BF16)
    left[:, : 2 * WIDTH] = left_in[...]
    late = jnp.where(at[0] == 0, late_recv[...], late_own[...])
    score_sum = sum(jnp.sum(block, axis=1, keepdims=True) for block in (early[...], soon[...], late))
    total, row_sum = product_of(left[...], rows[...].reshape(8 * WIDTH, HALF))
    row_sum = row_sum + rs_in[...]
    shift = score_sum * (1.0 / SCANS) - origin[:, :1]
    total = (total + total_in[...] - shift * row_sum) * (1.0 / (SCANS - 1))
    for c in range(8):
        parts[c] = total[:, c * 128 : (c + 1) * 128]
    means[...] = row_sum * (1.0 / SCANS)
    means_part[...] = means[:, pl.ds(pl.multiple_of(column[0] * 128, 128), 128)]


def last_part(at, column, own, recv, state):
    return pl.pallas_call(
        last_kernel,
        out_shape=[
            jax.ShapeDtypeStruct((8, COMPS, 128), F32),
            jax.ShapeDtypeStruct((1, HALF), F32),
            jax.ShapeDtypeStruct((1, 128), F32),
        ],
        in_specs=[IN_SMEM] * 2 + [IN_VMEM] * 14,
        out_specs=[IN_VMEM] * 3,
        scratch_shapes=[
            pltpu.VMEM((64, LOCAL, HALF), BF16),
            pltpu.VMEM((2 * COMPS + 16, 8 * WIDTH), BF16),
        ],
        compiler_params=MIDDLE,
        cost_estimate=pl.CostEstimate(flops=4 << 30, bytes_accessed=4 << 20, transcendentals=0),
    )(at, column, *own, *recv, *state)


def gram_kernel(at, *refs):
    own, recv, row_means, out = refs[:3], refs[3:6], refs[6], refs[7]
    rows, cols, stage, col_sums, sems, out_sems = refs[8:]
    fetch(at[0], own, recv, rows, cols, sems)
    copies = []
    for i in range(4):
        slot = i % 2
        if i >= 2:
            copies[i - 2].wait()
        span_i = slice(i * 256, (i + 1) * 256)
        row_mean = jnp.transpose(jnp.broadcast_to(row_means[:, span_i], (128, 256)))[:, :1]
        if i == 0:
            for m in range(4):
                fetched(own, rows, cols, sems, m)
                left = ones_beside(rows[m, :, :, :, :, span_i].reshape(512, 256))
                for j in range(8):
                    span = slice(j * 256, (j + 1) * 256)
                    right = cols[m, :, :, :, :, span].reshape(512, 256)
                    both = lax.dot_general(left, right, LEFT, preferred_element_type=F32)
                    tile, col_sum = both[:256], both[256:257]
                    if m > 0:
                        tile += stage[slot, :, span]
                        col_sum += col_sums[:, span]
                    if m == 3:
                        tile = (tile - row_mean * col_sum) * (1.0 / (SCANS - 1))
                    stage[slot, :, span] = tile
                    col_sums[:, span] = col_sum
        else:
            left = rows[:, :, :, :, :, span_i].reshape(SCANS, 256)
            for j in range(8):
                span = slice(j * 256, (j + 1) * 256)
                right = cols[:, :, :, :, :, span].reshape(SCANS, 256)
                tile = lax.dot_general(left, right, LEFT, preferred_element_type=F32)
                stage[slot, :, span] = (tile - row_mean * col_sums[:, span]) * (1.0 / (SCANS - 1))
        copy = pltpu.make_async_copy(stage.at[slot], out.at[pl.ds(i * 256, 256), :], out_sems.at[slot])
        copy.start()
        copies.append(copy)
    for copy in copies[2:]:
        copy.wait()


def gram(at, own, recv, row_means):
    return pl.pallas_call(
        gram_kernel,
        out_shape=jax.ShapeDtypeStruct((HALF, PANEL), F32),
        in_specs=[IN_SMEM] + [ANY] * 6 + [IN_VMEM],
        out_specs=ANY,
        scratch_shapes=[
            ROWS,
            COLS,
            pltpu.VMEM((2, 256, PANEL), F32),
            pltpu.VMEM((1, PANEL), F32),
            pltpu.SemaphoreType.DMA((4,)),
            pltpu.SemaphoreType.DMA((2,)),
        ],
        compiler_params=pltpu.CompilerParams(vmem_limit_bytes=22 << 20),
        cost_estimate=pl.CostEstimate(flops=8 << 30, bytes_accessed=20 << 20, transcendentals=0),
    )(at, *[pltpu.with_memory_space_constraint(piece, pltpu.HBM) for piece in own + recv], row_means)


def add_up_kernel(parts, out):
    total = parts[0]
    for n in range(1, parts.shape[0]):
        total = total + parts[n]
    out[...] = total.T


def add_up(parts):
    return pl.pallas_call(
        add_up_kernel,
        out_shape=jax.ShapeDtypeStruct(parts.shape[:0:-1], F32),
        in_specs=[IN_VMEM],
        out_specs=IN_VMEM,
        compiler_params=SMALL,
    )(parts)


def scalar(value):
    return jnp.reshape(value, (1,)).astype(jnp.int32)


def on_device(patterns, components):
    row = lax.axis_index("brow")
    col = lax.axis_index("bcol")
    k, y, xh = row % 2, (row // 2) % 4, row // 8
    z, xl = col % 4, col // 4
    first = k == 0
    same = jnp.where(first, y, z)
    at = scalar(same)
    mine = pick(at, pltpu.with_memory_space_constraint(patterns, pltpu.HBM))
    sends = join(at, permute(patterns, swap), mine)
    got = {n: permute(sends[n], spread(STEPS[n])) for n in (3, 1, 2)}
    got = [sends[0]] + [got[n] for n in range(1, 4)]
    own_half = jnp.where(first, xh, xl)
    group_own, to_1, to_2, to_3 = group(scalar(k), scalar(own_half), got)
    at = scalar(k)
    near = [permute(to_1, across(1)), permute(to_3, across(3))]
    ring_own = [permute(group_own, around(d)) for d in STEPS[1:3]]
    near, ring_own, to_2 = lax.optimization_barrier((near, ring_own, to_2))
    far = permute(to_2, across(2))
    ring = pack((((0, 0, 2), (1, 0, 2), (2, 0, 1)), ((0, 0, 2), (1, 0, 2), (3, 1, 2))), *near, *ring_own)
    ring = [permute(ring[n], around(STEPS[n + 1])) for n in range(2)]
    (own_early,) = pack((tuple((n, 0, 2) for n in range(5)),), group_own, *ring_own, *near)
    own_early = own_early.reshape((5, 2, 4, LOCAL, PANEL))
    recv_early = permute(own_early, swap)
    *early, comps = early_part(at, own_early, recv_early, components)
    far, ring, early = lax.optimization_barrier((far, ring, early))
    late = pack((((0, 0, 2), (2, 0, 2)), ((1, 2, 4), (2, 0, 2))), *ring, far)
    opposite = permute(far, around(STEPS[3]))
    late = [permute(late[n], around(STEPS[n + 1])) for n in range(2)] + [opposite]
    (own_soon,) = pack((((0, 4, 5), (1, 4, 5), (0, 0, 4), (1, 0, 4), (2, 0, 2)),), *ring, far)
    own_soon = own_soon.reshape((6, 2, 4, LOCAL, PANEL))
    recv_soon = permute(own_soon, swap)
    soon = soon_part(at, (own_early, own_soon), (recv_early, recv_soon), comps, early)
    late, soon = lax.optimization_barrier((late, soon))
    (own_late,) = pack((((0, 0, 4), (1, 0, 4), (2, 0, 2)),), *late)
    own_late = own_late.reshape((5, 2, 4, LOCAL, PANEL))
    recv_late = permute(own_late, swap)
    own = [own_early, own_soon, own_late]
    recv = [recv_early, recv_soon, recv_late]
    scores = late_part(own_late, comps)
    parts, row_means, means_part = last_part(at, scalar(col), own, recv, (*early, *soon, scores, permute(scores, swap)))
    parts = lax.all_to_all(parts, "bcol", 0, 0, tiled=True)
    covariance = gram(at, own, recv, row_means)
    projected = add_up(parts)
    return covariance, projected, means_part[0]


def solution(mesh):
    return jax.shard_map(
        on_device,
        mesh=mesh,
        in_specs=(P(("brow", "bcol"), None), P("bcol", None)),
        out_specs=(P("brow", "bcol"), P(("brow", "bcol"), None), P(("brow", "bcol"))),
        check_vma=False,
    )
```
